32 devices in a mesh: dp: 16 (over z, y, core), feat: 2 (over x).
Axes of the slice: x: 2, y: 2, z: 4, core: 2. Of those that a mesh axis runs over, the one named last changes fastest.
Arguments:
- embeddings: bfloat16 [32768, 1024], P('dp', 'feat')
- assignments: int32 [32768], P('dp'), may hold values from 0 to 127, as said below
- order_index: int32 [32768], P('dp'), may hold values from 0 to 32767, each once
- cluster_blocks: int32 [128], replicated, may hold values from 1 to 4, as said below
Outputs:
- centroids: bfloat16 [128, 1024], P('dp', 'feat')
- centroid_sim: float32 [32768], P('dp')
- earlier_max: float32 [32768], P('dp')
The draws below stay inside these ranges and needn't reach their ends.
Inputs may be any that keep to these rules, and one draw needn't show every extreme that they name: `assignments`: every cluster holds at least one row. The rows of one index of dp name one cluster at most 32 times, and on every index some cluster exactly 32 times. `cluster_blocks`: the number of rows of the cluster divided by 128, rounded up; some cluster has 512 rows.
All inputs are finite; a program needn't handle non-finite values.
Results may differ from the reference program's by a relative error of at most 0.0012.
Values may be sent and summed in bfloat16 or wider, within the bound.
No kernel may reach another device: no remote copies, remote signals or barrier semaphores. Data moves between devices by JAX's collectives and lax.ppermute only.
A program may use at most 64 MiB of HBM per device.

```python
from functools import partial
import jax
import jax.numpy as jnp
from jax import lax

D = 1024
ROWS_DEV = 2048
BLOCK = 128
K = 128
ROWS = 32768
MOST = 32
CAPACITY = 512


def cluster_plan(key):
    devices = ROWS // ROWS_DEV
    slots = K * MOST
    hottest = max(1, K // 64)
    base_key = jax.random.fold_in(key, 101)
    key_weight, key_raw, key_hot, key_shuffle = jax.random.split(base_key, 4)
    weights = jax.random.randint(key_weight, (K,), 1, 9)
    raw = jax.random.randint(key_raw, (devices, K, MOST), 0, 8192) * weights[None, :, None]
    hot_order = jax.random.permutation(key_hot, K)
    is_hot = jnp.zeros((K,), jnp.int32).at[hot_order[:hottest]].set(1)
    device_ids = jnp.arange(devices)[:, None, None]
    cluster_ids = jnp.arange(K)[None, :, None]
    slot_ids = jnp.arange(MOST)[None, None, :]
    covers = (cluster_ids % devices == device_ids) & (slot_ids == 0)
    score = jnp.where(is_hot[None, :, None] == 1, 65538, jnp.where(covers, 65537, raw))
    distinct = score * slots + (cluster_ids * MOST + slot_ids)
    top_values, picked = lax.top_k(distinct.reshape(devices, slots), ROWS_DEV)
    chosen = (picked // MOST).astype(jnp.int32)
    chosen = jax.random.permutation(key_shuffle, chosen, axis=1, independent=True)
    return chosen.reshape(ROWS).astype(jnp.int32)


def draw_assignments(key, part):
    return cluster_plan(key)


def draw_cluster_blocks(key, part):
    clusters = cluster_plan(key)
    sizes = jax.ops.segment_sum(jnp.ones((ROWS,), jnp.int32), clusters, num_segments=K)
    return ((sizes + 127) // 128).astype(jnp.int32)


def draw_embeddings(key, part):
    clusters = cluster_plan(key)
    centre_key = jax.random.fold_in(key, 201)
    noise_key = jax.random.fold_in(key, 202)
    centres = jax.random.normal(centre_key, (K, D), jnp.float32)
    noise = jax.random.normal(noise_key, (ROWS, D), jnp.float32)
    values = 0.8 * centres[clusters] + noise
    return values.astype(jnp.bfloat16)


def setup_inputs(seed: int = 0) -> dict:
    splits = jax.random.split(jax.random.key(seed), 5)
    return {
        "embeddings": draw_embeddings(jax.random.fold_in(splits[4], 71), 0),
        "assignments": draw_assignments(jax.random.fold_in(splits[4], 71), 0),
        "order_index": jax.random.permutation(splits[2], ROWS).astype(jnp.int32),
        "cluster_blocks": draw_cluster_blocks(jax.random.fold_in(splits[4], 71), 0),
    }


epsilon = 1e-06

def masked_best(unit_rows, row_order, used_rows):
    leading = unit_rows[:used_rows]
    key_order = row_order[:used_rows]
    similar = jnp.dot(leading, leading.T, precision=lax.Precision.HIGHEST, preferred_element_type=jnp.float32)
    earlier = (key_order[None, :] < key_order[:, None]) & (key_order[None, :] >= 0)
    best_match = lax.optimization_barrier(jnp.max(jnp.where(earlier, similar, jnp.float32(-1.0)), axis=1))
    filler = jnp.full((unit_rows.shape[0] - used_rows,), -1.0, jnp.float32)
    return jnp.concatenate([best_match, filler])

def reference(embeddings, assignments, order_index, cluster_blocks):
    values = embeddings.astype(jnp.float32)
    counts_int = jax.ops.segment_sum(jnp.ones((ROWS,), jnp.int32), assignments, num_segments=K)
    counts = counts_int.astype(jnp.float32)
    sums = jax.ops.segment_sum(values, assignments, num_segments=K)
    averages = sums / counts[:, None]
    centre_norms = lax.optimization_barrier(jnp.sum(averages * averages, axis=1))
    centroids = (averages / jnp.sqrt(centre_norms + epsilon)[:, None]).astype(jnp.bfloat16)
    squares = lax.optimization_barrier(jnp.sum(values * values, axis=1))
    products = lax.optimization_barrier(jnp.sum(values * centroids[assignments].astype(jnp.float32), axis=1))
    lengths = jnp.sqrt(squares + epsilon)
    centroid_sim = products / lengths
    unit_rows = (values / lengths[:, None]).astype(jnp.bfloat16)
    sort_order = jnp.argsort(assignments, stable=True).astype(jnp.int32)
    sorted_rows = unit_rows[sort_order].astype(jnp.float32)
    sorted_order = order_index[sort_order]
    sorted_cluster = assignments[sort_order]
    first_slot = (jnp.cumsum(counts_int) - counts_int).astype(jnp.int32)
    padded_rows = jnp.concatenate([sorted_rows, jnp.zeros((CAPACITY, D), jnp.float32)])
    padded_order = jnp.concatenate([sorted_order, jnp.full((CAPACITY,), -1, jnp.int32)])
    branches = [partial(masked_best, used_rows=(level + 1) * BLOCK) for level in range(CAPACITY // BLOCK)]

    def one_cluster(cluster):
        begin = first_slot[cluster]
        rows_here = lax.dynamic_slice_in_dim(padded_rows, begin, CAPACITY, 0)
        order_here = lax.dynamic_slice_in_dim(padded_order, begin, CAPACITY, 0)
        order_here = jnp.where(jnp.arange(CAPACITY, dtype=jnp.int32) < counts_int[cluster], order_here, -1)
        return lax.switch(cluster_blocks[cluster] - 1, branches, rows_here, order_here)
    results = lax.map(one_cluster, jnp.arange(K, dtype=jnp.int32))
    within = jnp.arange(ROWS, dtype=jnp.int32) - first_slot[sorted_cluster]
    sorted_best = results.reshape(-1)[sorted_cluster * CAPACITY + within]
    earlier_max = jnp.zeros((ROWS,), jnp.float32).at[sort_order].set(sorted_best)
    return (centroids, centroid_sim, earlier_max)
```

```python
from functools import partial

import jax
import jax.numpy as jnp
from jax import lax
from jax.experimental import pallas as pl
from jax.experimental.pallas import tpu as pltpu
from jax.sharding import PartitionSpec as P

epsilon = 1e-06
lanes = 128
AXES = ("dp", "feat")
f32 = jnp.float32
bf16 = jnp.bfloat16
last_last = (((1,), (1,)), ((), ()))


def iota(shape, dim):
    return lax.broadcasted_iota(jnp.int32, shape, dim)


def pack_kernel(
    dests, slots, assign_ref, order_ref, blocks_ref, rows_ref, out_ref, info_ref, table_ref,
    flat_ref, pieces_ref, places_ref, meta_ref,
):
    clusters = blocks_ref.shape[1]
    rows = rows_ref.shape[0]
    width = rows_ref.shape[1]
    share = clusters // dests
    cap = slots - 1

    sort_key = (blocks_ref[...] * clusters + iota((1, clusters), 1)).astype(f32)
    key_cols = jnp.broadcast_to(sort_key, (clusters, clusters))
    key_rows = key_cols.T
    rank = jnp.sum(jnp.where(key_cols < key_rows, 1.0, 0.0), axis=1, keepdims=True)
    turn = sum(jnp.where(rank >= t * dests, 1.0, 0.0) for t in range(1, share))
    rest = rank - turn * dests
    odd = (turn == 1.0) | (turn == 3.0)
    dest_of = jnp.where(odd, dests - 1.0 - rest, rest)
    code_of = dest_of * share + turn
    table_ref[...] = jnp.broadcast_to(code_of, table_ref.shape).astype(jnp.int32)

    step = 2 * lanes
    before = (iota((step, step), 0) < iota((step, step), 1)).astype(f32).astype(bf16)
    taken = jnp.zeros((dests, 1), f32)
    for b in range(rows // step):
        at = pl.ds(b * step, step)
        assign = jnp.concatenate([assign_ref[2 * b : 2 * b + 1], assign_ref[2 * b + 1 : 2 * b + 2]], axis=1)
        order = jnp.concatenate([order_ref[2 * b : 2 * b + 1], order_ref[2 * b + 1 : 2 * b + 2]], axis=1)
        member = iota((clusters, step), 0) == assign
        code = jnp.sum(jnp.where(member, code_of, 0.0), axis=0, keepdims=True).astype(jnp.int32)
        dest = code // share
        turn_row = code - dest * share
        hit = iota((dests, step), 0) == dest
        hit_f = jnp.where(hit, 1.0, 0.0)
        ahead = jnp.dot(hit_f.astype(bf16), before, preferred_element_type=f32) + taken
        taken = taken + jnp.sum(hit_f, axis=1, keepdims=True)
        position = jnp.sum(jnp.where(hit, ahead, 0.0), axis=0, keepdims=True).astype(jnp.int32)
        info_ref[0:1, at] = dest
        info_ref[1:2, at] = position
        fits = position < cap
        flat_ref[0:1, at] = jnp.where(fits, dest * slots + position, -1)
        parts = (order & 127, (order >> 7) & 127, order >> 14, turn_row + 1)
        for q, part in enumerate(parts):
            pieces_ref[q * dests : (q + 1) * dests, at] = jnp.where(hit, part.astype(f32), 0.0).astype(bf16)
        places_ref[:, at] = jnp.where((iota((lanes, step), 0) == position) & fits, 1.0, 0.0).astype(bf16)

    meta = lax.dot_general(pieces_ref[...], places_ref[...], last_last, preferred_element_type=f32)
    if cap < lanes:
        most = jnp.max(taken, axis=0, keepdims=True)
        flagged = (iota(meta.shape, 0) >= 3 * dests) & (iota(meta.shape, 1) == lanes - 1)
        meta = jnp.where(flagged, most, meta)
    meta_ref[...] = meta

    group = max(1, 768 // slots)
    while dests % group:
        group -= 1
    flat = flat_ref[0:1, :]

    def place(g, _):
        base = g * group
        target = flat - base * slots
        hits = jnp.where(iota((group * slots, rows), 0) == target, 1.0, 0.0).astype(bf16)
        placed = jnp.dot(hits, rows_ref[...], preferred_element_type=f32)
        for j in range(group):
            note = jnp.concatenate(
                [meta_ref[pl.ds(q * dests + base + j, 1), :] for q in range(4)], axis=1
            )
            block = placed[j * slots : (j + 1) * slots]
            out_ref[base + j] = jnp.where(iota((slots, width), 0) == cap, note, block).astype(bf16)
        return 0

    lax.fori_loop(0, dests // group, place, 0)


def split3(value):
    high = value.astype(bf16).astype(f32)
    middle = (value - high).astype(bf16).astype(f32)
    return high, middle, value - high - middle


def owner_kernel(
    big, got_ref, back_ref, flag_ref, unit_ref, key_ref, low_ref, turn_ref, inverse_ref, row_key_ref, tile_ref, best_ref, centre_ref,
):
    blocks, slots, width = got_ref.shape
    sources = blocks // 2
    cap = slots - 1
    total = sources * slots
    lane = iota((1, lanes), 1)
    most = jnp.zeros((1, 1), f32)

    for s in range(sources):
        note = got_ref[2 * s, slots - 8 : slots, :].astype(f32)[7:8]
        turn = jnp.where(lane < cap, note[:, 3 * lanes : 4 * lanes], 0.0)
        order = note[:, :lanes] + 128.0 * note[:, lanes : 2 * lanes] + 16384.0 * note[:, 2 * lanes : 3 * lanes]
        if cap < lanes:
            most = jnp.maximum(most, note[:, 4 * lanes - 1 : 4 * lanes])
        turn_ref[s : s + 1, :] = turn
        key = jnp.where(turn > 0.0, turn * big + order, 0.0)
        tile_ref[s : s + 1, :] = key
        reach = min(slots, lanes)
        row_key_ref[0:1, s * slots : s * slots + reach] = key[:, :reach]
        if reach < slots:
            row_key_ref[0:1, s * slots + reach : (s + 1) * slots] = jnp.zeros((1, slots - reach), f32)
    flag_ref[...] = jnp.broadcast_to(jnp.where(most > cap, 1, 0), flag_ref.shape).astype(jnp.int32)
    key_cols = tile_ref[...].T
    turn_cols = turn_ref[...].T

    sums = [jnp.zeros((8, width), f32) for _ in range(2)]
    counts = jnp.zeros((8, 1), f32)
    for s in range(sources):
        at = pl.ds(s * slots, slots)
        key_col = key_cols[: min(slots, lanes), s : s + 1]
        turn_col = turn_cols[: min(slots, lanes), s : s + 1]
        turn_row = turn_ref[s : s + 1, : min(slots, lanes)]
        if slots > lanes:
            filler = jnp.zeros((slots - lanes, 1), f32)
            key_col = jnp.concatenate([key_col, filler], axis=0)
            turn_col = jnp.concatenate([turn_col, filler], axis=0)
        key_ref[at, :] = jnp.broadcast_to(key_col, (slots, lanes))
        low_ref[at, :] = jnp.broadcast_to(turn_col, (slots, lanes))
        first = got_ref[2 * s].astype(f32)
        second = got_ref[2 * s + 1].astype(f32)
        squares = jnp.sum(first * first + second * second, axis=1, keepdims=True)
        inverse = 1.0 / jnp.sqrt(squares + epsilon)
        inverse_ref[at, :] = jnp.broadcast_to(inverse, (slots, lanes))
        unit_ref[at, :width] = (first * inverse).astype(bf16)
        unit_ref[at, width:] = (second * inverse).astype(bf16)
        reach = min(slots, lanes)
        member = jnp.where(iota((8, reach), 0).astype(f32) == turn_row - 1.0, 1.0, 0.0)
        counts = counts + jnp.sum(member, axis=1, keepdims=True)
        member = member.astype(bf16)
        for f in range(2):
            sums[f] = sums[f] + jnp.dot(
                member, got_ref[2 * s + f, :reach, :], preferred_element_type=f32
            )

    counts = jnp.where(counts > 0.0, counts, 1.0)
    averages = [part / counts for part in sums]
    norms = jnp.sum(averages[0] * averages[0] + averages[1] * averages[1], axis=1, keepdims=True)
    lengths = jnp.sqrt(norms + epsilon)
    centres = [part / lengths for part in averages]
    for f in range(2):
        for j in range(4):
            for h in range(2):
                centre_ref[f, 2 * j + h : 2 * j + h + 1, :] = centres[f][j : j + 1, h * 256 : (h + 1) * 256]
    centres = [part.astype(bf16) for part in centres]

    group = max(1, 384 // slots)
    while sources % group:
        group -= 1
    span = group * slots

    def compare(g, _):
        start = pl.multiple_of(g * span, 8)
        mine = unit_ref[pl.ds(start, span), :]
        similar = lax.dot_general(mine, unit_ref[...], last_last, preferred_element_type=f32)
        own = key_ref[pl.ds(start, span), :][:, :1]
        low = low_ref[pl.ds(start, span), :][:, :1] * big
        other = row_key_ref[...]
        earlier = (other >= low) & (other < own)
        best = jnp.max(jnp.where(earlier, similar, -1.0), axis=1, keepdims=True)
        best_ref[pl.ds(start, span), :] = jnp.broadcast_to(best, (span, lanes))
        return 0

    lax.fori_loop(0, sources // group, compare, 0)

    lane_wide = iota((slots, lanes), 1)
    for s in range(sources):
        at = pl.ds(s * slots, slots)
        product = sum(
            lax.dot_general(got_ref[2 * s + f], centres[f], last_last, preferred_element_type=f32)
            for f in range(2)
        )
        chosen = iota((slots, 8), 1).astype(f32) == low_ref[at, :][:, :1] - 1.0
        cosine = jnp.sum(jnp.where(chosen, product, 0.0), axis=1, keepdims=True) * inverse_ref[at, :][:, :1]
        both = jnp.where(lane_wide == 0, cosine, best_ref[at, :])
        tile_ref[: min(slots, lanes), :] = both[:lanes]
        across = tile_ref[...].T
        parts = split3(across[0:1]) + split3(across[1:2])
        row = iota((8, lanes), 0)
        answer = jnp.zeros((8, lanes), f32)
        for t, part in enumerate(parts):
            answer = jnp.where(row == t, part, answer)
        for f in range(2):
            back_ref[2 * s + f] = jnp.concatenate([centre_ref[f], answer], axis=1).astype(bf16)


def return_kernel(share, mine_ref, back_ref, info_ref, table_ref, centre_ref, cosine_ref, best_ref):
    dests = back_ref.shape[0]
    rows = info_ref.shape[1]
    step = 4 * lanes
    answers = back_ref[:, :, 256:].reshape(dests * 8, lanes)
    for b in range(rows // step):
        at = pl.ds(b * step, step)
        dest = info_ref[0:1, at]
        position = info_ref[1:2, at]
        place = jnp.where(iota((lanes, step), 0) == position, 1.0, 0.0).astype(bf16)
        picked = jnp.dot(answers, place, preferred_element_type=f32)
        picked = jnp.where(iota((dests * 8, step), 0) // 8 == dest, picked, 0.0)
        picked = jnp.sum(picked.reshape(dests, 8, step), axis=0)
        cosine = picked[0:1] + picked[1:2] + picked[2:3]
        best = picked[3:4] + picked[4:5] + picked[5:6]
        for c in range(step // lanes):
            row = b * (step // lanes) + c
            cosine_ref[row : row + 1, :] = cosine[:, c * lanes : (c + 1) * lanes]
            best_ref[row : row + 1, :] = best[:, c * lanes : (c + 1) * lanes]
    owned = centre_ref.shape[0]
    code = table_ref[pl.ds(pl.multiple_of(mine_ref[0] * owned, 8), owned), :][:, :1]
    dest = code // share
    turn = code - dest * share
    stored = back_ref[:, :, :256].reshape(dests * 8, 256)
    for h in range(2):
        want = dest * 8 + 2 * turn + h
        hits = jnp.where(iota((owned, dests * 8), 1) == want, 1.0, 0.0).astype(bf16)
        centre_ref[:, h * 256 : (h + 1) * 256] = jnp.dot(
            hits, stored, preferred_element_type=f32
        ).astype(bf16)


def vmem(count):
    return [pl.BlockSpec(memory_space=pltpu.VMEM)] * count


params = pltpu.CompilerParams(vmem_limit_bytes=50 * 1024 * 1024)


def exchange(x):
    return lax.all_to_all(x, AXES, split_axis=0, concat_axis=0, tiled=True)


def route(slots, embeddings, assignments, order_index, cluster_blocks):
    n_dp = lax.axis_size("dp")
    dests = n_dp * lax.axis_size("feat")
    rows, width = embeddings.shape
    clusters = cluster_blocks.shape[0]
    share = clusters // dests
    total = n_dp * slots
    big = float(n_dp * rows)

    sent, info, table = pl.pallas_call(
        partial(pack_kernel, dests, slots),
        out_shape=(
            jax.ShapeDtypeStruct((dests, slots, width), bf16),
            jax.ShapeDtypeStruct((8, rows), jnp.int32),
            jax.ShapeDtypeStruct((clusters, lanes), jnp.int32),
        ),
        in_specs=vmem(4),
        out_specs=tuple(vmem(3)),
        scratch_shapes=[
            pltpu.VMEM((8, rows), jnp.int32),
            pltpu.VMEM((4 * dests, rows), bf16),
            pltpu.VMEM((lanes, rows), bf16),
            pltpu.VMEM((4 * dests, lanes), f32),
        ],
        compiler_params=params,
        name="pack",
    )(
        assignments.reshape(rows // lanes, lanes),
        order_index.reshape(rows // lanes, lanes),
        cluster_blocks.reshape(1, clusters),
        embeddings,
    )
    got = exchange(sent)
    back, flag = pl.pallas_call(
        partial(owner_kernel, big),
        out_shape=(
            jax.ShapeDtypeStruct((dests, 8, 384), bf16),
            jax.ShapeDtypeStruct((8, lanes), jnp.int32),
        ),
        in_specs=vmem(1),
        out_specs=tuple(vmem(2)),
        scratch_shapes=[
            pltpu.VMEM((total, 2 * width), bf16),
            pltpu.VMEM((total, lanes), f32),
            pltpu.VMEM((total, lanes), f32),
            pltpu.VMEM((lanes, lanes), f32),
            pltpu.VMEM((total, lanes), f32),
            pltpu.VMEM((1, total), f32),
            pltpu.VMEM((lanes, lanes), f32),
            pltpu.VMEM((total, lanes), f32),
            pltpu.VMEM((2, 8, 256), f32),
        ],
        compiler_params=params,
        name="owner",
    )(got)
    returned = exchange(back)
    mine = lax.axis_index("dp").reshape(1).astype(jnp.int32)
    centres, cosine, best = pl.pallas_call(
        partial(return_kernel, share),
        out_shape=(
            jax.ShapeDtypeStruct((clusters // n_dp, width), bf16),
            jax.ShapeDtypeStruct((rows // lanes, lanes), f32),
            jax.ShapeDtypeStruct((rows // lanes, lanes), f32),
        ),
        in_specs=[pl.BlockSpec(memory_space=pltpu.SMEM)] + vmem(3),
        out_specs=tuple(vmem(3)),
        compiler_params=params,
        name="answers",
    )(mine, returned, info, table)
    return (centres, cosine.reshape(rows), best.reshape(rows)), flag[0, 0] > 0


def body(embeddings, assignments, order_index, cluster_blocks):
    dests = lax.axis_size("dp") * lax.axis_size("feat")
    rows = assignments.shape[0]
    clusters = cluster_blocks.shape[0]
    most = (clusters // dests) * (2 * rows // clusters)
    args = (embeddings, assignments, order_index, cluster_blocks)
    outputs, over = route(3 * most // 4, *args)
    return lax.cond(over, lambda: route(most + 8, *args)[0], lambda: outputs)


def solution(mesh):
    return jax.shard_map(
        body,
        mesh=mesh,
        in_specs=(P("dp", "feat"), P("dp"), P("dp"), P()),
        out_specs=(P("dp", "feat"), P("dp"), P("dp")),
        check_vma=False,
    )
```

```python
from functools import partial

import jax
import jax.numpy as jnp
from jax import lax
from jax.experimental import pallas as pl
from jax.experimental.pallas import tpu as pltpu
from jax.sharding import PartitionSpec as P

epsilon = 1e-06
lanes = 128
band = 32
chunk = 512
AXES = ("dp", "feat")
f32 = jnp.float32
bf16 = jnp.bfloat16
last_last = (((1,), (1,)), ((), ()))


def iota(shape, dim):
    return lax.broadcasted_iota(jnp.int32, shape, dim)


def pack_kernel(
    dests, slots, assign_ref, order_ref, blocks_ref, rows_hbm, out_ref, info_ref, table_ref,
    rows_ref, pieces_ref, places_ref, hits_ref, total_ref, copy_sem,
):
    clusters = blocks_ref.shape[1]
    rows, width = rows_ref.shape
    share = clusters // dests
    cap = slots - 1
    tall = places_ref.shape[0]
    copy = pltpu.make_async_copy(rows_hbm, rows_ref, copy_sem)
    copy.start()

    sort_key = (blocks_ref[...] * clusters + iota((1, clusters), 1)).astype(f32)
    key_cols = jnp.broadcast_to(sort_key, (clusters, clusters))
    key_rows = key_cols.T
    rank = jnp.sum(jnp.where(key_cols < key_rows, 1.0, 0.0), axis=1, keepdims=True)
    turn = sum(jnp.where(rank >= t * dests, 1.0, 0.0) for t in range(1, share))
    rest = rank - turn * dests
    odd = (turn == 1.0) | (turn == 3.0)
    dest_of = jnp.where(odd, dests - 1.0 - rest, rest)
    code_of = dest_of * share + turn
    table_ref[...] = jnp.broadcast_to(code_of, table_ref.shape).astype(jnp.int32)

    step = 2 * lanes
    before = (iota((step, step), 0) < iota((step, step), 1)).astype(f32).astype(bf16)
    taken = jnp.zeros((dests, 1), f32)
    reach = []
    for b in range(rows // step):
        at = pl.ds(b * step, step)
        assign = jnp.concatenate([assign_ref[2 * b : 2 * b + 1], assign_ref[2 * b + 1 : 2 * b + 2]], axis=1)
        order = jnp.concatenate([order_ref[2 * b : 2 * b + 1], order_ref[2 * b + 1 : 2 * b + 2]], axis=1)
        member = iota((clusters, step), 0) == assign
        code = jnp.sum(jnp.where(member, code_of, 0.0), axis=0, keepdims=True).astype(jnp.int32)
        dest = code // share
        turn_row = code - dest * share
        hit = iota((dests, step), 0) == dest
        hit_f = jnp.where(hit, 1.0, 0.0)
        hits_ref[:, at] = hit_f
        ahead = jnp.dot(hit_f.astype(bf16), before, preferred_element_type=f32) + taken
        if b * step % chunk == 0:
            low = jnp.min(taken)
        taken = taken + jnp.sum(hit_f, axis=1, keepdims=True)
        if (b + 1) * step % chunk == 0:
            reach.append((low, jnp.max(taken)))
        position = jnp.sum(jnp.where(hit, ahead, 0.0), axis=0, keepdims=True).astype(jnp.int32)
        info_ref[0:1, at] = dest
        info_ref[1:2, at] = position
        fits = position < cap
        parts = (order & 127, (order >> 7) & 127, order >> 14, turn_row + 1)
        for q, part in enumerate(parts):
            pieces_ref[q * dests : (q + 1) * dests, at] = jnp.where(hit, part.astype(f32), 0.0).astype(bf16)
        places_ref[:, at] = jnp.where((iota((tall, step), 0) == position) & fits, 1.0, 0.0).astype(bf16)

    meta = lax.dot_general(pieces_ref[...], places_ref[:lanes, :], last_last, preferred_element_type=f32)
    if cap < lanes:
        most = jnp.max(taken, axis=0, keepdims=True)
        flagged = (iota(meta.shape, 0) >= 3 * dests) & (iota(meta.shape, 1) == lanes - 1)
        meta = jnp.where(flagged, most, meta)
    copy.wait()

    note = jnp.concatenate([meta[q * dests : (q + 1) * dests] for q in range(4)], axis=1)
    for p in range(0, slots, band):
        begin = sum(jnp.where(high <= p, 1, 0) for _, high in reach)
        end = sum(jnp.where(low < p + band, 1, 0) for low, _ in reach)
        total_ref[...] = jnp.zeros_like(total_ref)

        def add(c, _):
            at = pl.ds(pl.multiple_of(c * chunk, chunk), chunk)
            place = places_ref[p : p + band, at].astype(f32)
            hits = hits_ref[:, at][:, None, :] * place[None, :, :]
            hits = hits.reshape(dests * band, chunk).astype(bf16)
            total_ref[...] += jnp.dot(hits, rows_ref[at, :], preferred_element_type=f32)
            return 0

        lax.fori_loop(begin, end, add, 0)
        block = total_ref[...].reshape(dests, band, width)
        if p + band == slots:
            block = jnp.where(iota((dests, band, width), 1) == band - 1, note[:, None, :], block)
        out_ref[:, p : p + band, :] = block.astype(bf16)


def split3(value):
    high = value.astype(bf16).astype(f32)
    middle = (value - high).astype(bf16).astype(f32)
    return high, middle, value - high - middle


def owner_kernel(
    got_ref, back_ref, flag_ref, unit_ref, inverse_ref, order_ref, turn_ref, row_order_ref, row_turn_ref, row_best_ref, centre_ref,
):
    blocks, slots, width = got_ref.shape
    sources = blocks // 2
    cap = slots - 1
    reach = min(slots, lanes)
    lane = iota((1, lanes), 1)
    most = jnp.zeros((1, 1), f32)

    order_ref[...] = jnp.zeros_like(order_ref)
    turn_ref[...] = jnp.zeros_like(turn_ref)
    row_best_ref[...] = jnp.full(row_best_ref.shape, -1.0, f32)
    if reach < slots:
        row_turn_ref[...] = jnp.zeros_like(row_turn_ref)
        row_order_ref[...] = jnp.zeros_like(row_order_ref)
    for s in range(sources):
        note = got_ref[2 * s, slots - band : slots, :].astype(f32)[band - 1 :]
        turn = jnp.where(lane < cap, note[:, 3 * lanes : 4 * lanes], 0.0)
        order = note[:, :lanes] + 128.0 * note[:, lanes : 2 * lanes] + 16384.0 * note[:, 2 * lanes : 3 * lanes]
        if cap < lanes:
            most = jnp.maximum(most, note[:, 4 * lanes - 1 : 4 * lanes])
        turn_ref[s : s + 1, :] = turn
        order_ref[s : s + 1, :] = order
        row_turn_ref[0:1, s * slots : s * slots + reach] = turn[:, :reach]
        row_order_ref[0:1, s * slots : s * slots + reach] = order[:, :reach]
    flag_ref[...] = jnp.broadcast_to(jnp.where(most > cap, 1, 0), flag_ref.shape).astype(jnp.int32)
    order_cols = order_ref[...].T
    turn_cols = turn_ref[...].T

    def column(table, s):
        col = table[:reach, s : s + 1]
        if reach < slots:
            col = jnp.concatenate([col, jnp.zeros((slots - reach, 1), f32)], axis=0)
        return col

    group = max(1, 384 // slots)
    while sources % group:
        group -= 1
    span = group * slots
    sums = [jnp.zeros((8, width), f32) for _ in range(2)]
    counts = jnp.zeros((8, 1), f32)
    bests = []
    for g in range(sources // group):
        mine = pl.ds(g * span, span)
        for s in range(g * group, (g + 1) * group):
            at = pl.ds(s * slots, slots)
            first = got_ref[2 * s].astype(f32)
            second = got_ref[2 * s + 1].astype(f32)
            squares = jnp.sum(first * first + second * second, axis=1, keepdims=True)
            inverse = 1.0 / jnp.sqrt(squares + epsilon)
            inverse_ref[at, :] = inverse
            unit_ref[at, :width] = (first * inverse).astype(bf16)
            unit_ref[at, width:] = (second * inverse).astype(bf16)
            member = jnp.where(
                iota((8, reach), 0).astype(f32) == turn_ref[s : s + 1, :reach] - 1.0, 1.0, 0.0
            )
            counts = counts + jnp.sum(member, axis=1, keepdims=True)
            member = member.astype(bf16)
            for f in range(2):
                sums[f] = sums[f] + jnp.dot(
                    member, got_ref[2 * s + f, :reach, :], preferred_element_type=f32
                )
        turn_col = jnp.concatenate([column(turn_cols, s) for s in range(g * group, (g + 1) * group)], axis=0)
        order_col = jnp.concatenate([column(order_cols, s) for s in range(g * group, (g + 1) * group)], axis=0)
        units = unit_ref[mine, :]
        best = jnp.full((span, 1), -1.0, f32)
        for h in range(g + 1):
            theirs = pl.ds(h * span, span)
            similar = lax.dot_general(units, unit_ref[theirs, :], last_last, preferred_element_type=f32)
            similar = jnp.where(turn_col == row_turn_ref[0:1, theirs], similar, -1.0)
            earlier = row_order_ref[0:1, theirs] < order_col
            best = jnp.maximum(best, jnp.max(jnp.where(earlier, similar, -1.0), axis=1, keepdims=True))
            if h < g:
                other = jnp.max(jnp.where(earlier, -1.0, similar), axis=0, keepdims=True)
                row_best_ref[0:1, theirs] = jnp.maximum(row_best_ref[0:1, theirs], other)
        bests.append(best)

    counts = jnp.where(counts > 0.0, counts, 1.0)
    averages = [part / counts for part in sums]
    norms = jnp.sum(averages[0] * averages[0] + averages[1] * averages[1], axis=1, keepdims=True)
    lengths = jnp.sqrt(norms + epsilon)
    centres = [part / lengths for part in averages]
    for f in range(2):
        for j in range(4):
            for h in range(2):
                centre_ref[f, 2 * j + h : 2 * j + h + 1, :] = centres[f][j : j + 1, h * 256 : (h + 1) * 256]
    centres = [part.astype(bf16) for part in centres]

    cosines = jnp.zeros((reach, lanes), f32)
    table = jnp.zeros((reach, lanes), f32)
    lane_wide = iota((reach, lanes), 1)
    for s in range(sources):
        at = pl.ds(s * slots, slots)
        product = sum(
            lax.dot_general(got_ref[2 * s + f], centres[f], last_last, preferred_element_type=f32)
            for f in range(2)
        )
        chosen = iota((slots, 8), 1).astype(f32) == column(turn_cols, s) - 1.0
        cosine = jnp.sum(jnp.where(chosen, product, 0.0), axis=1, keepdims=True) * inverse_ref[at, :]
        best = bests[s // group][(s % group) * slots : (s % group) * slots + reach]
        table = jnp.where(lane_wide == s, cosine[:reach], table)
        table = jnp.where(lane_wide == sources + s, best, table)
    if reach < lanes:
        table = jnp.concatenate([table, jnp.zeros((lanes - reach, lanes), f32)], axis=0)
    across = table.T
    row_bests = [row_best_ref[0:1, s * slots : s * slots + reach] for s in range(sources)]
    if reach < lanes:
        filler = jnp.full((1, lanes - reach), -1.0, f32)
        row_bests = [jnp.concatenate([part, filler], axis=1) for part in row_bests]
    cosine_parts = split3(across[:sources])
    best_parts = split3(jnp.maximum(across[sources : 2 * sources], jnp.concatenate(row_bests, axis=0)))
    row = iota((8, lanes), 0)
    for s in range(sources):
        answer = jnp.zeros((8, lanes), f32)
        for t, part in enumerate(cosine_parts + best_parts):
            answer = jnp.where(row == t, part[s : s + 1], answer)
        for f in range(2):
            back_ref[2 * s + f] = jnp.concatenate([centre_ref[f], answer], axis=1).astype(bf16)


def return_kernel(share, mine_ref, back_ref, info_ref, table_ref, centre_ref, cosine_ref, best_ref):
    dests = back_ref.shape[0]
    rows = info_ref.shape[1]
    step = 4 * lanes
    answers = back_ref[:, :, 256:].reshape(dests * 8, lanes)
    for b in range(rows // step):
        at = pl.ds(b * step, step)
        dest = info_ref[0:1, at]
        position = info_ref[1:2, at]
        place = jnp.where(iota((lanes, step), 0) == position, 1.0, 0.0).astype(bf16)
        picked = jnp.dot(answers, place, preferred_element_type=f32)
        picked = jnp.where(iota((dests * 8, step), 0) // 8 == dest, picked, 0.0)
        picked = jnp.sum(picked.reshape(dests, 8, step), axis=0)
        cosine = picked[0:1] + picked[1:2] + picked[2:3]
        best = picked[3:4] + picked[4:5] + picked[5:6]
        for c in range(step // lanes):
            row = b * (step // lanes) + c
            cosine_ref[row : row + 1, :] = cosine[:, c * lanes : (c + 1) * lanes]
            best_ref[row : row + 1, :] = best[:, c * lanes : (c + 1) * lanes]
    owned = centre_ref.shape[0]
    code = table_ref[pl.ds(pl.multiple_of(mine_ref[0] * owned, 8), owned), :][:, :1]
    dest = code // share
    turn = code - dest * share
    stored = back_ref[:, :, :256].reshape(dests * 8, 256)
    for h in range(2):
        want = dest * 8 + 2 * turn + h
        hits = jnp.where(iota((owned, dests * 8), 1) == want, 1.0, 0.0).astype(bf16)
        centre_ref[:, h * 256 : (h + 1) * 256] = jnp.dot(
            hits, stored, preferred_element_type=f32
        ).astype(bf16)


def vmem(count):
    return [pl.BlockSpec(memory_space=pltpu.VMEM)] * count


params = pltpu.CompilerParams(vmem_limit_bytes=50 * 1024 * 1024)


def exchange(x):
    return lax.all_to_all(x, AXES, split_axis=0, concat_axis=0, tiled=True)


def route(slots, embeddings, assignments, order_index, cluster_blocks):
    n_dp = lax.axis_size("dp")
    dests = n_dp * lax.axis_size("feat")
    rows, width = embeddings.shape
    clusters = cluster_blocks.shape[0]
    share = clusters // dests
    total = n_dp * slots

    sent, info, table = pl.pallas_call(
        partial(pack_kernel, dests, slots),
        out_shape=(
            jax.ShapeDtypeStruct((dests, slots, width), bf16),
            jax.ShapeDtypeStruct((8, rows), jnp.int32),
            jax.ShapeDtypeStruct((clusters, lanes), jnp.int32),
        ),
        in_specs=vmem(3) + [pl.BlockSpec(memory_space=pl.ANY)],
        out_specs=tuple(vmem(3)),
        scratch_shapes=[
            pltpu.VMEM((rows, width), bf16),
            pltpu.VMEM((4 * dests, rows), bf16),
            pltpu.VMEM((max(lanes, slots), rows), bf16),
            pltpu.VMEM((dests, rows), f32),
            pltpu.VMEM((dests * band, width), f32),
            pltpu.SemaphoreType.DMA,
        ],
        compiler_params=params,
        name="pack",
    )(
        assignments.reshape(rows // lanes, lanes),
        order_index.reshape(rows // lanes, lanes),
        cluster_blocks.reshape(1, clusters),
        embeddings,
    )
    got = exchange(sent)
    back, flag = pl.pallas_call(
        owner_kernel,
        out_shape=(
            jax.ShapeDtypeStruct((dests, 8, 384), bf16),
            jax.ShapeDtypeStruct((8, lanes), jnp.int32),
        ),
        in_specs=vmem(1),
        out_specs=tuple(vmem(2)),
        scratch_shapes=[
            pltpu.VMEM((total, 2 * width), bf16),
            pltpu.VMEM((total, 1), f32),
            pltpu.VMEM((lanes, lanes), f32),
            pltpu.VMEM((lanes, lanes), f32),
            pltpu.VMEM((1, total), f32),
            pltpu.VMEM((1, total), f32),
            pltpu.VMEM((1, total), f32),
            pltpu.VMEM((2, 8, 256), f32),
        ],
        compiler_params=params,
        name="owner",
    )(got)
    returned = exchange(back)
    mine = lax.axis_index("dp").reshape(1).astype(jnp.int32)
    centres, cosine, best = pl.pallas_call(
        partial(return_kernel, share),
        out_shape=(
            jax.ShapeDtypeStruct((clusters // n_dp, width), bf16),
            jax.ShapeDtypeStruct((rows // lanes, lanes), f32),
            jax.ShapeDtypeStruct((rows // lanes, lanes), f32),
        ),
        in_specs=[pl.BlockSpec(memory_space=pltpu.SMEM)] + vmem(3),
        out_specs=tuple(vmem(3)),
        compiler_params=params,
        name="answers",
    )(mine, returned, info, table)
    return (centres, cosine.reshape(rows), best.reshape(rows)), flag[0, 0] > 0


def body(embeddings, assignments, order_index, cluster_blocks):
    dests = lax.axis_size("dp") * lax.axis_size("feat")
    rows = assignments.shape[0]
    clusters = cluster_blocks.shape[0]
    most = (clusters // dests) * (2 * rows // clusters)
    args = (embeddings, assignments, order_index, cluster_blocks)
    few = -(-3 * most // (4 * band)) * band
    outputs, over = route(few, *args)
    return lax.cond(over, lambda: route(most + band, *args)[0], lambda: outputs)


def solution(mesh):
    return jax.shard_map(
        body,
        mesh=mesh,
        in_specs=(P("dp", "feat"), P("dp"), P("dp"), P()),
        out_specs=(P("dp", "feat"), P("dp"), P("dp")),
        check_vma=False,
    )
```

```python
from functools import partial

import jax
import jax.numpy as jnp
from jax import lax
from jax.experimental import pallas as pl
from jax.experimental.pallas import tpu as pltpu
from jax.sharding import PartitionSpec as P

epsilon = 1e-06
lanes = 128
band = 32
chunk = 512
AXES = ("dp", "feat")
f32 = jnp.float32
bf16 = jnp.bfloat16
last_last = (((1,), (1,)), ((), ()))


def iota(shape, dim):
    return lax.broadcasted_iota(jnp.int32, shape, dim)


def deal_clusters(blocks, dests):
    clusters = blocks.shape[1]
    half = clusters // 2
    square = (clusters, clusters)
    here, there = iota(square, 0), iota(square, 1)
    together = (here >= half) == (there >= half)

    def counted(pairs, values=1.0):
        return jnp.where(pairs, values, 0.0)

    def down(table):
        return jnp.sum(table, axis=0, keepdims=True)

    def along(table):
        return jnp.sum(table, axis=1, keepdims=True)

    own_there = jnp.broadcast_to(blocks.astype(f32), square)
    own_here = own_there.T
    key_there = own_there * clusters + there.astype(f32)
    key_here = own_here * clusters + here.astype(f32)
    rank_here = along(counted(together & (key_there < key_here)))
    rank_there = down(counted(together & (key_here < key_there)))
    partner = together & (rank_here + rank_there == half - 1.0)

    def pair_key(own, other, rank):
        return (own + other) * clusters + jnp.minimum(rank, half - 1.0 - rank)

    pair_here = pair_key(own_here[:, :1], along(counted(partner, own_there)), rank_here)
    pair_there = pair_key(own_there[:1], down(counted(partner, own_here)), rank_there)
    spot = along(counted(together & (pair_there < pair_here), 0.5))
    is_upper = iota((clusters, 1), 0) >= half
    spot = jnp.where(is_upper, dests - 1.0 - spot, spot)
    turn = jnp.where(rank_here >= half // 2, 1.0, 0.0) + jnp.where(is_upper, 2.0, 0.0)
    return spot * 4.0 + turn


def pack_kernel(
    dests, slots, assign_ref, order_ref, blocks_ref, rows_hbm, out_ref, info_ref, table_ref,
    rows_ref, pieces_ref, places_ref, hits_ref, copy_sem,
):
    clusters = blocks_ref.shape[1]
    rows, width = rows_ref.shape
    share = 4
    cap = slots - 1
    tall = places_ref.shape[0]
    copy = pltpu.make_async_copy(rows_hbm, rows_ref, copy_sem)
    copy.start()

    code_of = deal_clusters(blocks_ref[...], dests)
    table_ref[...] = jnp.broadcast_to(code_of, table_ref.shape).astype(jnp.int32)

    step = 2 * lanes
    before = (iota((step, step), 0) < iota((step, step), 1)).astype(f32).astype(bf16)
    taken = jnp.zeros((dests, 1), f32)
    reach = []
    for b in range(rows // step):
        at = pl.ds(b * step, step)
        assign = jnp.concatenate([assign_ref[2 * b : 2 * b + 1], assign_ref[2 * b + 1 : 2 * b + 2]], axis=1)
        order = jnp.concatenate([order_ref[2 * b : 2 * b + 1], order_ref[2 * b + 1 : 2 * b + 2]], axis=1)
        member = iota((clusters, step), 0) == assign
        code = jnp.sum(jnp.where(member, code_of, 0.0), axis=0, keepdims=True).astype(jnp.int32)
        dest = code // share
        turn_row = code - dest * share
        hit = iota((dests, step), 0) == dest
        hit_f = jnp.where(hit, 1.0, 0.0)
        hits_ref[:, at] = hit_f
        ahead = jnp.dot(hit_f.astype(bf16), before, preferred_element_type=f32) + taken
        if b * step % chunk == 0:
            low = jnp.min(taken)
        taken = taken + jnp.sum(hit_f, axis=1, keepdims=True)
        if (b + 1) * step % chunk == 0:
            reach.append((low, jnp.max(taken)))
        position = jnp.sum(jnp.where(hit, ahead, 0.0), axis=0, keepdims=True).astype(jnp.int32)
        info_ref[0:1, at] = dest
        info_ref[1:2, at] = position
        fits = position < cap
        parts = (order & 127, (order >> 7) & 127, order >> 14, turn_row + 1)
        for q, part in enumerate(parts):
            pieces_ref[q * dests : (q + 1) * dests, at] = jnp.where(hit, part.astype(f32), 0.0).astype(bf16)
        places_ref[:, at] = jnp.where((iota((tall, step), 0) == position) & fits, 1.0, 0.0).astype(bf16)

    meta = lax.dot_general(pieces_ref[...], places_ref[:lanes, :], last_last, preferred_element_type=f32)
    if cap < lanes:
        most = jnp.max(taken, axis=0, keepdims=True)
        flagged = (iota(meta.shape, 0) >= 3 * dests) & (iota(meta.shape, 1) == lanes - 1)
        meta = jnp.where(flagged, most, meta)
    copy.wait()

    note = jnp.concatenate([meta[q * dests : (q + 1) * dests] for q in range(4)], axis=1)
    for p in range(0, slots, band):
        begin = sum(jnp.where(high <= p, 1, 0) for _, high in reach)
        end = sum(jnp.where(low < p + band, 1, 0) for low, _ in reach)
        out_ref[:, p : p + band, :] = jnp.zeros((dests, band, width), bf16)

        def add(c, _):
            at = pl.ds(pl.multiple_of(c * chunk, chunk), chunk)
            place = places_ref[p : p + band, at]
            hits = jnp.concatenate(
                [
                    jnp.broadcast_to(hits_ref[d : d + 1, at], (16, chunk)).astype(bf16) * place[r : r + 16]
                    for d in range(dests)
                    for r in range(0, band, 16)
                ],
                axis=0,
            )
            placed = jnp.dot(hits, rows_ref[at, :], preferred_element_type=f32).astype(bf16)
            out_ref[:, p : p + band, :] += placed.reshape(dests, band, width)
            return 0

        lax.fori_loop(begin, end, add, 0)
    last = out_ref[:, slots - 16 :, :]
    last = jnp.where(iota(last.shape, 1) == 15, note.astype(bf16)[:, None, :], last)
    out_ref[:, slots - 16 :, :] = last


def split3(value):
    high = value.astype(bf16).astype(f32)
    middle = (value - high).astype(bf16).astype(f32)
    return high, middle, value - high - middle


def owner_kernel(
    got_ref, back_ref, flag_ref, unit_ref, inverse_ref, order_ref, turn_ref, row_order_ref, row_turn_ref, row_best_ref, centre_ref,
):
    blocks, slots, width = got_ref.shape
    sources = blocks // 2
    cap = slots - 1
    reach = min(slots, lanes)
    lane = iota((1, lanes), 1)
    most = jnp.zeros((1, 1), f32)

    order_ref[...] = jnp.zeros_like(order_ref)
    turn_ref[...] = jnp.zeros_like(turn_ref)
    row_best_ref[...] = jnp.full(row_best_ref.shape, -1.0, f32)
    if reach < slots:
        row_turn_ref[...] = jnp.zeros_like(row_turn_ref)
        row_order_ref[...] = jnp.zeros_like(row_order_ref)
    for s in range(sources):
        note = got_ref[2 * s, slots - band : slots, :].astype(f32)[band - 1 :]
        turn = jnp.where(lane < cap, note[:, 3 * lanes : 4 * lanes], 0.0)
        order = note[:, :lanes] + 128.0 * note[:, lanes : 2 * lanes] + 16384.0 * note[:, 2 * lanes : 3 * lanes]
        if cap < lanes:
            most = jnp.maximum(most, note[:, 4 * lanes - 1 : 4 * lanes])
        turn_ref[s : s + 1, :] = turn
        order_ref[s : s + 1, :] = order
        row_turn_ref[0:1, s * slots : s * slots + reach] = turn[:, :reach]
        row_order_ref[0:1, s * slots : s * slots + reach] = order[:, :reach]
    flag_ref[...] = jnp.broadcast_to(jnp.where(most > cap, 1, 0), flag_ref.shape).astype(jnp.int32)
    order_cols = order_ref[...].T
    turn_cols = turn_ref[...].T

    def column(table, s):
        col = table[:reach, s : s + 1]
        if reach < slots:
            col = jnp.concatenate([col, jnp.zeros((slots - reach, 1), f32)], axis=0)
        return col

    group = max(1, 384 // slots)
    while sources % group:
        group -= 1
    span = group * slots
    sums = [jnp.zeros((8, width), f32) for _ in range(2)]
    counts = jnp.zeros((8, 1), f32)
    bests = []
    for g in range(sources // group):
        mine = pl.ds(g * span, span)
        for s in range(g * group, (g + 1) * group):
            at = pl.ds(s * slots, slots)
            first = got_ref[2 * s].astype(f32)
            second = got_ref[2 * s + 1].astype(f32)
            squares = jnp.sum(first * first + second * second, axis=1, keepdims=True)
            inverse = 1.0 / jnp.sqrt(squares + epsilon)
            inverse_ref[at, :] = inverse
            unit_ref[at, :width] = (first * inverse).astype(bf16)
            unit_ref[at, width:] = (second * inverse).astype(bf16)
            member = jnp.where(
                iota((8, reach), 0).astype(f32) == turn_ref[s : s + 1, :reach] - 1.0, 1.0, 0.0
            )
            counts = counts + jnp.sum(member, axis=1, keepdims=True)
            member = member.astype(bf16)
            for f in range(2):
                sums[f] = sums[f] + jnp.dot(
                    member, got_ref[2 * s + f, :reach, :], preferred_element_type=f32
                )
        turn_col = jnp.concatenate([column(turn_cols, s) for s in range(g * group, (g + 1) * group)], axis=0)
        order_col = jnp.concatenate([column(order_cols, s) for s in range(g * group, (g + 1) * group)], axis=0)
        units = unit_ref[mine, :]
        near = pl.ds(0, (g + 1) * span)
        similar = lax.dot_general(units, unit_ref[near, :], last_last, preferred_element_type=f32)
        similar = jnp.where(turn_col == row_turn_ref[0:1, near], similar, -1.0)
        earlier = row_order_ref[0:1, near] < order_col
        best = jnp.max(jnp.where(earlier, similar, -1.0), axis=1, keepdims=True)
        if g:
            before = pl.ds(0, g * span)
            later = jnp.where(earlier[:, : g * span], -1.0, similar[:, : g * span])
            row_best_ref[0:1, before] = jnp.maximum(
                row_best_ref[0:1, before], jnp.max(later, axis=0, keepdims=True)
            )
        bests.append(best)

    counts = jnp.where(counts > 0.0, counts, 1.0)
    averages = [part / counts for part in sums]
    norms = jnp.sum(averages[0] * averages[0] + averages[1] * averages[1], axis=1, keepdims=True)
    lengths = jnp.sqrt(norms + epsilon)
    centres = [part / lengths for part in averages]
    for f in range(2):
        for j in range(4):
            for h in range(4):
                row = 4 * (j % 2) + h
                centre_ref[2 * (j // 2) + f, row : row + 1, :] = centres[f][j : j + 1, h * lanes : (h + 1) * lanes]
    centres = [part.astype(bf16) for part in centres]

    cosines = []
    table = jnp.zeros((reach, lanes), f32)
    lane_wide = iota((reach, lanes), 1)
    for s in range(sources):
        product = sum(
            lax.dot_general(centres[f], got_ref[2 * s + f, :reach, :], last_last, preferred_element_type=f32)
            for f in range(2)
        )
        chosen = iota((8, reach), 0).astype(f32) == turn_ref[s : s + 1, :reach] - 1.0
        cosines.append(jnp.sum(jnp.where(chosen, product, 0.0), axis=0, keepdims=True))
        inverse = inverse_ref[s * slots : s * slots + reach, :]
        best = bests[s // group][(s % group) * slots : (s % group) * slots + reach]
        table = jnp.where(lane_wide == s, inverse, table)
        table = jnp.where(lane_wide == sources + s, best, table)
    if reach < lanes:
        table = jnp.concatenate([table, jnp.zeros((lanes - reach, lanes), f32)], axis=0)
        cosines = [jnp.concatenate([part, jnp.zeros((1, lanes - reach), f32)], axis=1) for part in cosines]
    across = table.T
    row_bests = [row_best_ref[0:1, s * slots : s * slots + reach] for s in range(sources)]
    if reach < lanes:
        filler = jnp.full((1, lanes - reach), -1.0, f32)
        row_bests = [jnp.concatenate([part, filler], axis=1) for part in row_bests]
    cosine_parts = split3(jnp.concatenate(cosines, axis=0) * across[:sources])
    best_parts = split3(jnp.maximum(across[sources : 2 * sources], jnp.concatenate(row_bests, axis=0)))
    row = iota((8, lanes), 0)
    for s in range(sources):
        answer = jnp.zeros((8, lanes), f32)
        for t, part in enumerate(cosine_parts + best_parts):
            answer = jnp.where(row == t, part[s : s + 1], answer)
        for f in range(2):
            back_ref[2 * s + f] = jnp.concatenate([centre_ref[2 * (2 * s // sources) + f], answer], axis=1).astype(bf16)


def return_kernel(share, mine_ref, back_ref, info_ref, table_ref, centre_ref, cosine_ref, best_ref):
    dests = back_ref.shape[0]
    rows = info_ref.shape[1]
    step = 4 * lanes
    answers = back_ref[:, :, lanes:].reshape(dests * 8, lanes)
    for b in range(rows // step):
        at = pl.ds(b * step, step)
        dest = info_ref[0:1, at]
        position = info_ref[1:2, at]
        place = jnp.where(iota((lanes, step), 0) == position, 1.0, 0.0).astype(bf16)
        picked = jnp.dot(answers, place, preferred_element_type=f32)
        picked = jnp.where(iota((dests * 8, step), 0) // 8 == dest, picked, 0.0)
        picked = jnp.sum(picked.reshape(dests, 8, step), axis=0)
        cosine = picked[0:1] + picked[1:2] + picked[2:3]
        best = picked[3:4] + picked[4:5] + picked[5:6]
        for c in range(step // lanes):
            row = b * (step // lanes) + c
            cosine_ref[row : row + 1, :] = cosine[:, c * lanes : (c + 1) * lanes]
            best_ref[row : row + 1, :] = best[:, c * lanes : (c + 1) * lanes]
    owned = centre_ref.shape[0]
    code = table_ref[pl.ds(pl.multiple_of(mine_ref[0] * owned, 8), owned), :][:, :1]
    dest = code // share
    turn = code - dest * share
    stored = back_ref[:, :, :lanes].reshape(dests * 8, lanes)
    for h in range(4):
        want = dest * 8 + 4 * (turn % 2) + h
        hits = jnp.where(iota((owned, dests * 8), 1) == want, 1.0, 0.0).astype(bf16)
        centre_ref[:, h * lanes : (h + 1) * lanes] = jnp.dot(
            hits, stored, preferred_element_type=f32
        ).astype(bf16)


def vmem(count):
    return [pl.BlockSpec(memory_space=pltpu.VMEM)] * count


params = pltpu.CompilerParams(vmem_limit_bytes=50 * 1024 * 1024)


def exchange(x):
    return lax.all_to_all(x, AXES, split_axis=0, concat_axis=0, tiled=True)


def route(slots, embeddings, assignments, order_index, cluster_blocks):
    n_dp = lax.axis_size("dp")
    dests = n_dp * lax.axis_size("feat")
    rows, width = embeddings.shape
    clusters = cluster_blocks.shape[0]
    share = clusters // dests
    total = n_dp * slots

    sent, info, table = pl.pallas_call(
        partial(pack_kernel, dests, slots),
        out_shape=(
            jax.ShapeDtypeStruct((dests, slots, width), bf16),
            jax.ShapeDtypeStruct((8, rows), jnp.int32),
            jax.ShapeDtypeStruct((clusters, lanes), jnp.int32),
        ),
        in_specs=vmem(3) + [pl.BlockSpec(memory_space=pl.ANY)],
        out_specs=tuple(vmem(3)),
        scratch_shapes=[
            pltpu.VMEM((rows, width), bf16),
            pltpu.VMEM((4 * dests, rows), bf16),
            pltpu.VMEM((max(lanes, slots), rows), bf16),
            pltpu.VMEM((dests, rows), f32),
            pltpu.SemaphoreType.DMA,
        ],
        compiler_params=params,
        name="pack",
    )(
        assignments.reshape(rows // lanes, lanes),
        order_index.reshape(rows // lanes, lanes),
        cluster_blocks.reshape(1, clusters),
        embeddings,
    )
    got = exchange(sent)
    back, flag = pl.pallas_call(
        owner_kernel,
        out_shape=(
            jax.ShapeDtypeStruct((dests, 8, 2 * lanes), bf16),
            jax.ShapeDtypeStruct((8, lanes), jnp.int32),
        ),
        in_specs=vmem(1),
        out_specs=tuple(vmem(2)),
        scratch_shapes=[
            pltpu.VMEM((total, 2 * width), bf16),
            pltpu.VMEM((total, 1), f32),
            pltpu.VMEM((lanes, lanes), f32),
            pltpu.VMEM((lanes, lanes), f32),
            pltpu.VMEM((1, total), f32),
            pltpu.VMEM((1, total), f32),
            pltpu.VMEM((1, total), f32),
            pltpu.VMEM((4, 8, lanes), f32),
        ],
        compiler_params=params,
        name="owner",
    )(got)
    returned = exchange(back)
    mine = lax.axis_index("dp").reshape(1).astype(jnp.int32)
    centres, cosine, best = pl.pallas_call(
        partial(return_kernel, share),
        out_shape=(
            jax.ShapeDtypeStruct((clusters // n_dp, width), bf16),
            jax.ShapeDtypeStruct((rows // lanes, lanes), f32),
            jax.ShapeDtypeStruct((rows // lanes, lanes), f32),
        ),
        in_specs=[pl.BlockSpec(memory_space=pltpu.SMEM)] + vmem(3),
        out_specs=tuple(vmem(3)),
        compiler_params=params,
        name="answers",
    )(mine, returned, info, table)
    return (centres, cosine.reshape(rows), best.reshape(rows)), flag[0, 0] > 0


def body(embeddings, assignments, order_index, cluster_blocks):
    dests = lax.axis_size("dp") * lax.axis_size("feat")
    rows = assignments.shape[0]
    clusters = cluster_blocks.shape[0]
    most = (clusters // dests) * (2 * rows // clusters)
    args = (embeddings, assignments, order_index, cluster_blocks)
    few = -(-3 * most // (4 * band)) * band
    outputs, over = route(few, *args)
    return lax.cond(over, lambda: route(most + band, *args)[0], lambda: outputs)


def solution(mesh):
    return jax.shard_map(
        body,
        mesh=mesh,
        in_specs=(P("dp", "feat"), P("dp"), P("dp"), P()),
        out_specs=(P("dp", "feat"), P("dp"), P("dp")),
        check_vma=False,
    )
```

```python
from functools import partial

import jax
import jax.numpy as jnp
from jax import lax
from jax.experimental import pallas as pl
from jax.experimental.pallas import tpu as pltpu
from jax.sharding import PartitionSpec as P

epsilon = 1e-06
lanes = 128
band = 32
chunk = 512
AXES = ("dp", "feat")
f32 = jnp.float32
bf16 = jnp.bfloat16
last_last = (((1,), (1,)), ((), ()))


def iota(shape, dim):
    return lax.broadcasted_iota(jnp.int32, shape, dim)


def deal_clusters(blocks, dests):
    clusters = blocks.shape[1]
    half = clusters // 2
    square = (clusters, clusters)
    here, there = iota(square, 0), iota(square, 1)
    together = (here >= half) == (there >= half)

    def counted(pairs, values=1.0):
        return jnp.where(pairs, values, 0.0)

    def down(table):
        return jnp.sum(table, axis=0, keepdims=True)

    def along(table):
        return jnp.sum(table, axis=1, keepdims=True)

    own_there = jnp.broadcast_to(blocks.astype(f32), square)
    own_here = own_there.T
    key_there = own_there * clusters + there.astype(f32)
    key_here = own_here * clusters + here.astype(f32)
    rank_here = along(counted(together & (key_there < key_here)))
    rank_there = down(counted(together & (key_here < key_there)))
    partner = together & (rank_here + rank_there == half - 1.0)

    def pair_key(own, other, rank):
        return (own + other) * clusters + jnp.minimum(rank, half - 1.0 - rank)

    pair_here = pair_key(own_here[:, :1], along(counted(partner, own_there)), rank_here)
    pair_there = pair_key(own_there[:1], down(counted(partner, own_here)), rank_there)
    spot = along(counted(together & (pair_there < pair_here), 0.5))
    is_upper = iota((clusters, 1), 0) >= half
    spot = jnp.where(is_upper, dests - 1.0 - spot, spot)
    turn = jnp.where(rank_here >= half // 2, 1.0, 0.0) + jnp.where(is_upper, 2.0, 0.0)
    return spot * 4.0 + turn


def pack_kernel(
    dests, slots, spare, assign_ref, order_ref, blocks_ref, rows_hbm, out_ref, info_ref, table_ref,
    rows_ref, pieces_ref, noted_ref, places_ref, hits_ref, copy_sem,
):
    clusters = blocks_ref.shape[1]
    rows, width = rows_ref.shape
    share = 4
    cap = slots - 1
    copy = pltpu.make_async_copy(rows_hbm, rows_ref, copy_sem)
    copy.start()

    code_of = deal_clusters(blocks_ref[...], dests)
    table_ref[...] = jnp.broadcast_to(code_of, table_ref.shape).astype(jnp.int32)

    step = 2 * lanes
    steps = rows // step
    before = jnp.where(iota((step, step), 0) < iota((step, step), 1), 1.0, 0.0).astype(bf16)

    def row(ref, b):
        return jnp.concatenate([ref[2 * b : 2 * b + 1], ref[2 * b + 1 : 2 * b + 2]], axis=1)

    codes, hits = [], []
    for b in range(steps):
        member = iota((clusters, step), 0) == row(assign_ref, b)
        code = jnp.sum(jnp.where(member, code_of, 0.0), axis=0, keepdims=True).astype(jnp.int32)
        codes.append(code)
        hits.append(jnp.where(iota((dests, step), 0) == code // 4, 1.0, 0.0))
    stacked = jnp.concatenate(hits, axis=0)
    ahead = jnp.dot(stacked.astype(bf16), before, preferred_element_type=f32)
    held = jnp.sum(stacked, axis=1, keepdims=True)
    taken = jnp.zeros((dests, 1), f32)
    reach = []
    for b in range(steps):
        at = pl.ds(b * step, step)
        mine = slice(b * dests, (b + 1) * dests)
        if b * step % chunk == 0:
            low = jnp.min(taken)
        place = jnp.sum(hits[b] * (ahead[mine] + taken), axis=0, keepdims=True)
        taken = taken + held[mine]
        if (b + 1) * step % chunk == 0:
            reach.append((low, jnp.max(taken)))
        dest = codes[b] // 4
        position = place.astype(jnp.int32)
        info_ref[0:1, at] = dest
        info_ref[1:2, at] = position
        if spare:
            over = position >= cap
            target = jnp.where(over, dest ^ 2, dest)
            there = jnp.where(over, jnp.where(position < cap + spare, position - spare, -1), position)
            hits_ref[:, at] = jnp.where(iota((dests, step), 0) == target, 1.0, 0.0)
        else:
            there = jnp.where(position < cap, position, -1)
            hits_ref[:, at] = hits[b]
        order = row(order_ref, b)
        parts = (order & 127, (order >> 7) & 127, order >> 14, codes[b] - dest * 4 + 1)
        for q, part in enumerate(parts):
            pieces_ref[q * dests : (q + 1) * dests, at] = (hits[b] * part.astype(f32)).astype(bf16)
        noted_ref[:, at] = jnp.where(iota((lanes, step), 0) == position, 1.0, 0.0).astype(bf16)
        places_ref[:, at] = jnp.where(iota((places_ref.shape[0], step), 0) == there, 1.0, 0.0).astype(bf16)

    meta = lax.dot_general(pieces_ref[...], noted_ref[...], last_last, preferred_element_type=f32)
    if spare:
        square = (dests, dests)
        loads = jnp.broadcast_to(taken, square).T
        sibling = jnp.sum(
            jnp.where(iota(square, 1) == (iota(square, 0) ^ 2), loads, 0.0), axis=1, keepdims=True
        )
        over = taken > cap
        stuck = over & ((taken > cap + spare) | (sibling > cap - spare))
        level = jnp.where(over, 1.0, 0.0) + jnp.where(stuck, 1.0, 0.0)
        level = jnp.max(level, axis=0, keepdims=True)
        flagged = (iota(meta.shape, 0) >= 3 * dests) & (iota(meta.shape, 1) == lanes - 1)
        meta = jnp.where(flagged, level, meta)
    copy.wait()

    note = jnp.concatenate([meta[q * dests : (q + 1) * dests] for q in range(4)], axis=1)
    for p in range(0, slots, band):
        tall = min(band, slots - p)
        begin = sum(jnp.where(high <= p, 1, 0) for _, high in reach)
        end = sum(jnp.where(low < p + tall, 1, 0) for low, _ in reach)
        out_ref[:, p : p + tall, :] = jnp.zeros((dests, tall, width), bf16)

        def add(c, _):
            at = pl.ds(pl.multiple_of(c * chunk, chunk), chunk)
            place = places_ref[p : p + tall, at]
            hits = jnp.concatenate(
                [
                    jnp.broadcast_to(hits_ref[d : d + 1, at], (min(16, tall - r), chunk)).astype(bf16)
                    * place[r : r + 16]
                    for d in range(dests)
                    for r in range(0, tall, 16)
                ],
                axis=0,
            )
            placed = jnp.dot(hits, rows_ref[at, :], preferred_element_type=f32).astype(bf16)
            out_ref[:, p : p + tall, :] += placed.reshape(dests, tall, width)
            return 0

        lax.fori_loop(begin, end, add, 0)
    at = pl.ds(p, tall)
    last = out_ref[:, at, :]
    last = jnp.where(iota(last.shape, 1) == tall - 1, note.astype(bf16)[:, None, :], last)
    out_ref[:, at, :] = last


def split3(value):
    high = value.astype(bf16).astype(f32)
    middle = (value - high).astype(bf16).astype(f32)
    return high, middle, value - high - middle


def owner_kernel(spare, got_ref, *refs):
    more_ref, refs = (refs[0], refs[1:]) if spare else (None, refs)
    back_ref, flag_ref, unit_ref, inverse_ref, order_ref, turn_ref, *refs = refs
    row_order_ref, row_turn_ref, row_best_ref, centre_ref = refs
    blocks, sent, width = got_ref.shape
    sources = blocks // 2
    cap = sent - 1
    slots = sent + 16 if spare else sent
    shift = 16 - spare
    reach = min(slots, lanes)
    lane = iota((1, lanes), 1)
    moved = (lane >= cap + shift) & (lane < cap + shift + spare)

    def block(s, f):
        if spare:
            both = got_ref[2 * s + f].astype(f32), more_ref[2 * s + f].astype(f32)
            return jnp.concatenate(both, axis=0).astype(bf16)
        return got_ref[2 * s + f]

    def by_slot(values):
        kept = jnp.where(lane < cap, values, 0.0)
        return jnp.where(moved, pltpu.roll(values, shift, 1), kept) if spare else kept

    most = jnp.zeros((1, 1), f32)

    order_ref[...] = jnp.zeros_like(order_ref)
    turn_ref[...] = jnp.zeros_like(turn_ref)
    row_best_ref[...] = jnp.full(row_best_ref.shape, -1.0, f32)
    if reach < slots:
        row_turn_ref[...] = jnp.zeros_like(row_turn_ref)
        row_order_ref[...] = jnp.zeros_like(row_order_ref)
    for s in range(sources):
        note = got_ref[2 * s, cap // 16 * 16 :, :].astype(f32)[cap % 16 :]
        turn = by_slot(note[:, 3 * lanes : 4 * lanes])
        order = by_slot(
            note[:, :lanes] + 128.0 * note[:, lanes : 2 * lanes] + 16384.0 * note[:, 2 * lanes : 3 * lanes]
        )
        if cap < lanes:
            most = jnp.maximum(most, note[:, 4 * lanes - 1 : 4 * lanes])
        turn_ref[s : s + 1, :] = turn
        order_ref[s : s + 1, :] = order
        row_turn_ref[0:1, s * slots : s * slots + reach] = turn[:, :reach]
        row_order_ref[0:1, s * slots : s * slots + reach] = order[:, :reach]
    flag_ref[...] = jnp.broadcast_to(most, flag_ref.shape).astype(jnp.int32)
    order_cols = order_ref[...].T
    turn_cols = turn_ref[...].T

    def column(table, s):
        col = table[:reach, s : s + 1]
        if reach < slots:
            col = jnp.concatenate([col, jnp.zeros((slots - reach, 1), f32)], axis=0)
        return col

    group = max(1, 416 // slots)
    while sources % group:
        group -= 1
    span = group * slots
    sums = [jnp.zeros((8, width), f32) for _ in range(2)]
    counts = jnp.zeros((8, 1), f32)
    bests, cosines = [], []
    for g in range(sources // group):
        mine = pl.ds(g * span, span)
        for s in range(g * group, (g + 1) * group):
            at = pl.ds(s * slots, slots)
            raw = block(s, 0), block(s, 1)
            first = raw[0].astype(f32)
            second = raw[1].astype(f32)
            squares = jnp.sum(first * first + second * second, axis=1, keepdims=True)
            inverse = 1.0 / jnp.sqrt(squares + epsilon)
            inverse_ref[at, :] = inverse
            unit_ref[at, :width] = (first * inverse).astype(bf16)
            unit_ref[at, width:] = (second * inverse).astype(bf16)
            member = jnp.where(
                iota((8, reach), 0).astype(f32) == turn_ref[s : s + 1, :reach] - 1.0, 1.0, 0.0
            )
            counts = counts + jnp.sum(member, axis=1, keepdims=True)
            member = member.astype(bf16)
            for f in range(2):
                sums[f] = sums[f] + jnp.dot(
                    member, raw[f][:reach], preferred_element_type=f32
                )
        turn_col = jnp.concatenate([column(turn_cols, s) for s in range(g * group, (g + 1) * group)], axis=0)
        order_col = jnp.concatenate([column(order_cols, s) for s in range(g * group, (g + 1) * group)], axis=0)
        if (g + 1) * group == sources:
            counts = jnp.where(counts > 0.0, counts, 1.0)
            averages = [part / counts for part in sums]
            norms = jnp.sum(averages[0] * averages[0] + averages[1] * averages[1], axis=1, keepdims=True)
            lengths = jnp.sqrt(norms + epsilon)
            centres = [part / lengths for part in averages]
            for f in range(2):
                for j in range(4):
                    for h in range(4):
                        row = 4 * (j % 2) + h
                        centre_ref[2 * (j // 2) + f, row : row + 1, :] = centres[f][j : j + 1, h * lanes : (h + 1) * lanes]
            centres = [part.astype(bf16) for part in centres]

            for s in range(sources):
                product = sum(
                    lax.dot_general(centres[f], block(s, f)[:reach], last_last, preferred_element_type=f32)
                    for f in range(2)
                )
                chosen = iota((8, reach), 0).astype(f32) == turn_ref[s : s + 1, :reach] - 1.0
                cosines.append(jnp.sum(jnp.where(chosen, product, 0.0), axis=0, keepdims=True))
        units = unit_ref[mine, :]
        near = pl.ds(0, (g + 1) * span)
        similar = lax.dot_general(units, unit_ref[near, :], last_last, preferred_element_type=f32)
        similar = jnp.where(turn_col == row_turn_ref[0:1, near], similar, -1.0)
        earlier = row_order_ref[0:1, near] < order_col
        best = jnp.max(jnp.where(earlier, similar, -1.0), axis=1, keepdims=True)
        if g:
            before = pl.ds(0, g * span)
            later = jnp.where(earlier[:, : g * span], -1.0, similar[:, : g * span])
            row_best_ref[0:1, before] = jnp.maximum(
                row_best_ref[0:1, before], jnp.max(later, axis=0, keepdims=True)
            )
        bests.append(best)

    table = jnp.zeros((reach, lanes), f32)
    lane_wide = iota((reach, lanes), 1)
    for s in range(sources):
        inverse = inverse_ref[s * slots : s * slots + reach, :]
        best = bests[s // group][(s % group) * slots : (s % group) * slots + reach]
        table = jnp.where(lane_wide == s, inverse, table)
        table = jnp.where(lane_wide == sources + s, best, table)
    if reach < lanes:
        table = jnp.concatenate([table, jnp.zeros((lanes - reach, lanes), f32)], axis=0)
        cosines = [jnp.concatenate([part, jnp.zeros((1, lanes - reach), f32)], axis=1) for part in cosines]
    across = table.T
    row_bests = [row_best_ref[0:1, s * slots : s * slots + reach] for s in range(sources)]
    if reach < lanes:
        filler = jnp.full((1, lanes - reach), -1.0, f32)
        row_bests = [jnp.concatenate([part, filler], axis=1) for part in row_bests]
    cosine = jnp.concatenate(cosines, axis=0) * across[:sources]
    best = jnp.maximum(across[sources : 2 * sources], jnp.concatenate(row_bests, axis=0))
    if spare:
        cosine = jnp.where(lane < cap, cosine, pltpu.roll(cosine, lanes - shift, 1))
        best = jnp.where(lane < cap, best, pltpu.roll(best, lanes - shift, 1))
    cosine_parts = split3(cosine)
    best_parts = split3(best)
    row = iota((8, lanes), 0)
    for s in range(sources):
        answer = jnp.zeros((8, lanes), f32)
        for t, part in enumerate(cosine_parts + best_parts):
            answer = jnp.where(row == t, part[s : s + 1], answer)
        for f in range(2):
            back_ref[2 * s + f] = jnp.concatenate([centre_ref[2 * (2 * s // sources) + f], answer], axis=1).astype(bf16)


def return_kernel(share, mine_ref, back_ref, info_ref, table_ref, centre_ref, cosine_ref, best_ref):
    dests = back_ref.shape[0]
    rows = info_ref.shape[1]
    step = 4 * lanes
    answers = back_ref[:, :, lanes:].reshape(dests * 8, lanes)
    for b in range(rows // step):
        at = pl.ds(b * step, step)
        dest = info_ref[0:1, at]
        position = info_ref[1:2, at]
        place = jnp.where(iota((lanes, step), 0) == position, 1.0, 0.0).astype(bf16)
        picked = jnp.dot(answers, place, preferred_element_type=f32)
        picked = jnp.where(iota((dests * 8, step), 0) // 8 == dest, picked, 0.0)
        picked = jnp.sum(picked.reshape(dests, 8, step), axis=0)
        cosine = picked[0:1] + picked[1:2] + picked[2:3]
        best = picked[3:4] + picked[4:5] + picked[5:6]
        for c in range(step // lanes):
            row = b * (step // lanes) + c
            cosine_ref[row : row + 1, :] = cosine[:, c * lanes : (c + 1) * lanes]
            best_ref[row : row + 1, :] = best[:, c * lanes : (c + 1) * lanes]
    owned = centre_ref.shape[0]
    code = table_ref[pl.ds(pl.multiple_of(mine_ref[0] * owned, 8), owned), :][:, :1]
    dest = code // share
    turn = code - dest * share
    stored = back_ref[:, :, :lanes].reshape(dests * 8, lanes)
    for h in range(4):
        want = dest * 8 + 4 * (turn % 2) + h
        hits = jnp.where(iota((owned, dests * 8), 1) == want, 1.0, 0.0).astype(bf16)
        centre_ref[:, h * lanes : (h + 1) * lanes] = jnp.dot(
            hits, stored, preferred_element_type=f32
        ).astype(bf16)


def vmem(count):
    return [pl.BlockSpec(memory_space=pltpu.VMEM)] * count


params = pltpu.CompilerParams(vmem_limit_bytes=50 * 1024 * 1024)


def exchange(x):
    return lax.all_to_all(x, AXES, split_axis=0, concat_axis=0, tiled=True)


def send(slots, spare, embeddings, assignments, order_index, cluster_blocks):
    dests = lax.axis_size("dp") * lax.axis_size("feat")
    rows, width = embeddings.shape
    clusters = cluster_blocks.shape[0]
    sent, info, table = pl.pallas_call(
        partial(pack_kernel, dests, slots, spare),
        out_shape=(
            jax.ShapeDtypeStruct((dests, slots, width), bf16),
            jax.ShapeDtypeStruct((8, rows), jnp.int32),
            jax.ShapeDtypeStruct((clusters, lanes), jnp.int32),
        ),
        in_specs=vmem(3) + [pl.BlockSpec(memory_space=pl.ANY)],
        out_specs=tuple(vmem(3)),
        scratch_shapes=[
            pltpu.VMEM((rows, width), bf16),
            pltpu.VMEM((4 * dests, rows), bf16),
            pltpu.VMEM((lanes, rows), bf16),
            pltpu.VMEM((-(-slots // 16) * 16, rows), bf16),
            pltpu.VMEM((dests, rows), f32),
            pltpu.SemaphoreType.DMA,
        ],
        compiler_params=params,
        name="pack",
    )(
        assignments.reshape(rows // lanes, lanes),
        order_index.reshape(rows // lanes, lanes),
        cluster_blocks.reshape(1, clusters),
        embeddings,
    )
    return exchange(sent), info, table


def answer(spare, got, info, table):
    n_dp = lax.axis_size("dp")
    dests, slots, width = got[0].shape
    total = n_dp * sum(part.shape[1] for part in got)
    rows = info.shape[1]
    back, level = pl.pallas_call(
        partial(owner_kernel, spare),
        out_shape=(
            jax.ShapeDtypeStruct((dests, 8, 2 * lanes), bf16),
            jax.ShapeDtypeStruct((8, lanes), jnp.int32),
        ),
        in_specs=vmem(len(got)),
        out_specs=tuple(vmem(2)),
        scratch_shapes=[
            pltpu.VMEM((total, 2 * width), bf16),
            pltpu.VMEM((total, 1), f32),
            pltpu.VMEM((lanes, lanes), f32),
            pltpu.VMEM((lanes, lanes), f32),
            pltpu.VMEM((1, total), f32),
            pltpu.VMEM((1, total), f32),
            pltpu.VMEM((1, total), f32),
            pltpu.VMEM((4, 8, lanes), f32),
        ],
        compiler_params=params,
        name="owner",
    )(*got)
    returned = exchange(back)
    mine = lax.axis_index("dp").reshape(1).astype(jnp.int32)
    centres, cosine, best = pl.pallas_call(
        partial(return_kernel, 4),
        out_shape=(
            jax.ShapeDtypeStruct((table.shape[0] // n_dp, width), bf16),
            jax.ShapeDtypeStruct((rows // lanes, lanes), f32),
            jax.ShapeDtypeStruct((rows // lanes, lanes), f32),
        ),
        in_specs=[pl.BlockSpec(memory_space=pltpu.SMEM)] + vmem(3),
        out_specs=tuple(vmem(3)),
        compiler_params=params,
        name="answers",
    )(mine, returned, info, table)
    return (centres, cosine.reshape(rows), best.reshape(rows)), level[0, 0]


def body(embeddings, assignments, order_index, cluster_blocks):
    n_dp = lax.axis_size("dp")
    dests = n_dp * lax.axis_size("feat")
    rows = assignments.shape[0]
    clusters = cluster_blocks.shape[0]
    most = (clusters // dests) * (2 * rows // clusters)
    args = (embeddings, assignments, order_index, cluster_blocks)
    few = -(-11 * most // 128) * 8
    got, info, table = send(few, 8, *args)
    outputs, level = answer(0, (got,), info, table)

    def with_sibling():
        more = lax.ppermute(got[:, few - 16 :], "dp", [(i, i ^ 1) for i in range(n_dp)])
        return answer(8, (got, more), info, table)[0]

    def with_all():
        got, info, table = send(most + 32, 0, *args)
        return answer(0, (got,), info, table)[0]

    return lax.switch(level, [lambda: outputs, with_sibling, with_all])


def solution(mesh):
    return jax.shard_map(
        body,
        mesh=mesh,
        in_specs=(P("dp", "feat"), P("dp"), P("dp"), P()),
        out_specs=(P("dp", "feat"), P("dp"), P("dp")),
        check_vma=False,
    )
```

```python
from functools import partial

import jax
import jax.numpy as jnp
from jax import lax
from jax.experimental import pallas as pl
from jax.experimental.pallas import tpu as pltpu
from jax.sharding import PartitionSpec as P

epsilon = 1e-06
lanes = 128
band = 32
chunk = 512
AXES = ("dp", "feat")
f32 = jnp.float32
bf16 = jnp.bfloat16
last_last = (((1,), (1,)), ((), ()))


def iota(shape, dim):
    return lax.broadcasted_iota(jnp.int32, shape, dim)


def deal_clusters(blocks, dests):
    clusters = blocks.shape[1]
    half = clusters // 2
    square = (clusters, clusters)
    here, there = iota(square, 0), iota(square, 1)
    together = (here >= half) == (there >= half)

    def counted(pairs, values=1.0):
        return jnp.where(pairs, values, 0.0)

    def down(table):
        return jnp.sum(table, axis=0, keepdims=True)

    def along(table):
        return jnp.sum(table, axis=1, keepdims=True)

    own_there = jnp.broadcast_to(blocks.astype(f32), square)
    own_here = own_there.T
    key_there = own_there * clusters + there.astype(f32)
    key_here = own_here * clusters + here.astype(f32)
    rank_here = along(counted(together & (key_there < key_here)))
    rank_there = down(counted(together & (key_here < key_there)))
    partner = together & (rank_here + rank_there == half - 1.0)

    def pair_key(own, other, rank):
        return (own + other) * clusters + jnp.minimum(rank, half - 1.0 - rank)

    pair_here = pair_key(own_here[:, :1], along(counted(partner, own_there)), rank_here)
    pair_there = pair_key(own_there[:1], down(counted(partner, own_here)), rank_there)
    spot = along(counted(together & (pair_there < pair_here), 0.5))
    is_upper = iota((clusters, 1), 0) >= half
    spot = jnp.where(is_upper, dests - 1.0 - spot, spot)
    turn = jnp.where(rank_here >= half // 2, 1.0, 0.0) + jnp.where(is_upper, 2.0, 0.0)
    return spot * 4.0 + turn


def pack_kernel(
    dests, slots, spare, assign_ref, order_ref, blocks_ref, rows_hbm, out_ref, info_ref, table_ref,
    rows_ref, pieces_ref, noted_ref, places_ref, hits_ref, copy_sem,
):
    clusters = blocks_ref.shape[1]
    rows, width = rows_ref.shape
    share = 4
    cap = slots - 1
    copy = pltpu.make_async_copy(rows_hbm, rows_ref, copy_sem)
    copy.start()

    code_of = deal_clusters(blocks_ref[...], dests)
    table_ref[...] = jnp.broadcast_to(code_of, table_ref.shape).astype(jnp.int32)

    step = 2 * lanes
    steps = rows // step
    before = jnp.where(iota((step, step), 0) < iota((step, step), 1), 1.0, 0.0).astype(bf16)

    def row(ref, b):
        return jnp.concatenate([ref[2 * b : 2 * b + 1], ref[2 * b + 1 : 2 * b + 2]], axis=1)

    codes, hits = [], []
    for b in range(steps):
        member = iota((clusters, step), 0) == row(assign_ref, b)
        code = jnp.sum(jnp.where(member, code_of, 0.0), axis=0, keepdims=True).astype(jnp.int32)
        codes.append(code)
        hits.append(jnp.where(iota((dests, step), 0) == code // 4, 1.0, 0.0))
    stacked = jnp.concatenate(hits, axis=0)
    ahead = jnp.dot(stacked.astype(bf16), before, preferred_element_type=f32)
    held = jnp.sum(stacked, axis=1, keepdims=True)
    taken = jnp.zeros((dests, 1), f32)
    reach = []
    for b in range(steps):
        at = pl.ds(b * step, step)
        mine = slice(b * dests, (b + 1) * dests)
        if b * step % chunk == 0:
            low = jnp.min(taken)
        place = jnp.sum(hits[b] * (ahead[mine] + taken), axis=0, keepdims=True)
        taken = taken + held[mine]
        if (b + 1) * step % chunk == 0:
            reach.append((low, jnp.max(taken)))
        dest = codes[b] // 4
        position = place.astype(jnp.int32)
        info_ref[0:1, at] = dest
        info_ref[1:2, at] = position
        if spare:
            over = position >= cap
            target = jnp.where(over, dest ^ 2, dest)
            there = jnp.where(over, jnp.where(position < cap + spare, position - spare, -1), position)
            hits_ref[:, at] = jnp.where(iota((dests, step), 0) == target, 1.0, 0.0)
        else:
            there = jnp.where(position < cap, position, -1)
            hits_ref[:, at] = hits[b]
        order = row(order_ref, b)
        parts = (order & 127, (order >> 7) & 127, order >> 14, codes[b] - dest * 4 + 1)
        for q, part in enumerate(parts):
            pieces_ref[q * dests : (q + 1) * dests, at] = (hits[b] * part.astype(f32)).astype(bf16)
        noted_ref[:, at] = jnp.where(iota((lanes, step), 0) == position, 1.0, 0.0).astype(bf16)
        places_ref[:, at] = jnp.where(iota((places_ref.shape[0], step), 0) == there, 1.0, 0.0).astype(bf16)

    meta = lax.dot_general(pieces_ref[...], noted_ref[...], last_last, preferred_element_type=f32)
    if spare:
        square = (dests, dests)
        loads = jnp.broadcast_to(taken, square).T
        sibling = jnp.sum(
            jnp.where(iota(square, 1) == (iota(square, 0) ^ 2), loads, 0.0), axis=1, keepdims=True
        )
        over = taken > cap
        stuck = over & ((taken > cap + spare) | (sibling > cap - spare))
        level = jnp.where(over, 1.0, 0.0) + jnp.where(stuck, 1.0, 0.0)
        level = jnp.max(level, axis=0, keepdims=True)
        flagged = (iota(meta.shape, 0) >= 3 * dests) & (iota(meta.shape, 1) == lanes - 1)
        meta = jnp.where(flagged, level, meta)
    copy.wait()

    note = jnp.concatenate([meta[q * dests : (q + 1) * dests] for q in range(4)], axis=1)
    for p in range(0, slots, band):
        tall = min(band, slots - p)
        begin = sum(jnp.where(high <= p, 1, 0) for _, high in reach)
        end = sum(jnp.where(low < p + tall, 1, 0) for low, _ in reach)
        out_ref[:, p : p + tall, :] = jnp.zeros((dests, tall, width), bf16)

        def add(c, _):
            at = pl.ds(pl.multiple_of(c * chunk, chunk), chunk)
            place = places_ref[p : p + tall, at]
            hits = jnp.concatenate(
                [
                    jnp.broadcast_to(hits_ref[d : d + 1, at], (min(16, tall - r), chunk)).astype(bf16)
                    * place[r : r + 16]
                    for d in range(dests)
                    for r in range(0, tall, 16)
                ],
                axis=0,
            )
            placed = jnp.dot(hits, rows_ref[at, :], preferred_element_type=f32).astype(bf16)
            out_ref[:, p : p + tall, :] += placed.reshape(dests, tall, width)
            return 0

        lax.fori_loop(begin, end, add, 0)
    at = pl.ds(p, tall)
    last = out_ref[:, at, :]
    last = jnp.where(iota(last.shape, 1) == tall - 1, note.astype(bf16)[:, None, :], last)
    out_ref[:, at, :] = last


def split3(value):
    high = value.astype(bf16).astype(f32)
    middle = (value - high).astype(bf16).astype(f32)
    return high, middle, value - high - middle


def owner_kernel(spare, got_ref, *refs):
    more_ref, refs = (refs[0], refs[1:]) if spare else (None, refs)
    back_ref, flag_ref, unit_ref, inverse_ref, order_ref, turn_ref, *refs = refs
    row_order_ref, row_turn_ref, row_best_ref, centre_ref = refs
    blocks, sent, width = got_ref.shape
    sources = blocks // 2
    cap = sent - 1
    slots = sent + 16 if spare else sent
    shift = 16 - spare
    reach = min(slots, lanes)
    lane = iota((1, lanes), 1)
    moved = (lane >= cap + shift) & (lane < cap + shift + spare)

    def block(s, f):
        if spare:
            both = got_ref[2 * s + f].astype(f32), more_ref[2 * s + f].astype(f32)
            return jnp.concatenate(both, axis=0).astype(bf16)
        return got_ref[2 * s + f]

    def by_slot(values):
        kept = jnp.where(lane < cap, values, 0.0)
        return jnp.where(moved, pltpu.roll(values, shift, 1), kept) if spare else kept

    most = jnp.zeros((1, 1), f32)

    order_ref[...] = jnp.zeros_like(order_ref)
    turn_ref[...] = jnp.zeros_like(turn_ref)
    row_best_ref[...] = jnp.full(row_best_ref.shape, -1.0, f32)
    if reach < slots:
        row_turn_ref[...] = jnp.zeros_like(row_turn_ref)
        row_order_ref[...] = jnp.zeros_like(row_order_ref)
    for s in range(sources):
        note = got_ref[2 * s, cap // 16 * 16 :, :].astype(f32)[cap % 16 :]
        turn = by_slot(note[:, 3 * lanes : 4 * lanes])
        order = by_slot(
            note[:, :lanes] + 128.0 * note[:, lanes : 2 * lanes] + 16384.0 * note[:, 2 * lanes : 3 * lanes]
        )
        if cap < lanes:
            most = jnp.maximum(most, note[:, 4 * lanes - 1 : 4 * lanes])
        turn_ref[s : s + 1, :] = turn
        order_ref[s : s + 1, :] = order
        row_turn_ref[0:1, s * slots : s * slots + reach] = turn[:, :reach]
        row_order_ref[0:1, s * slots : s * slots + reach] = order[:, :reach]
    flag_ref[...] = jnp.broadcast_to(most, flag_ref.shape).astype(jnp.int32)
    order_cols = order_ref[...].T
    turn_cols = turn_ref[...].T

    def column(table, s):
        col = table[:reach, s : s + 1]
        if reach < slots:
            col = jnp.concatenate([col, jnp.zeros((slots - reach, 1), f32)], axis=0)
        return col

    group = max(1, 416 // slots)
    while sources % group:
        group -= 1
    span = group * slots
    sums = [jnp.zeros((8, width), f32) for _ in range(2)]
    counts = jnp.zeros((8, 1), f32)
    bests, cosines = [], []
    for g in range(sources // group):
        mine = pl.ds(g * span, span)
        for s in range(g * group, (g + 1) * group, 2):
            at = pl.ds(s * slots, 2 * slots)
            raw = [[block(s + i, f) for f in range(2)] for i in range(2)]
            first, second = [
                jnp.concatenate([raw[0][f].astype(f32), raw[1][f].astype(f32)], axis=0) for f in range(2)
            ]
            squares = jnp.sum(first * first + second * second, axis=1, keepdims=True)
            inverse = 1.0 / jnp.sqrt(squares + epsilon)
            inverse_ref[at, :] = inverse
            unit_ref[at, :width] = (first * inverse).astype(bf16)
            unit_ref[at, width:] = (second * inverse).astype(bf16)
            for i in range(2):
                member = jnp.where(
                    iota((8, reach), 0).astype(f32) == turn_ref[s + i : s + i + 1, :reach] - 1.0, 1.0, 0.0
                )
                counts = counts + jnp.sum(member, axis=1, keepdims=True)
                member = member.astype(bf16)
                for f in range(2):
                    sums[f] = sums[f] + jnp.dot(
                        member, raw[i][f][:reach], preferred_element_type=f32
                    )
        turn_col = jnp.concatenate([column(turn_cols, s) for s in range(g * group, (g + 1) * group)], axis=0)
        order_col = jnp.concatenate([column(order_cols, s) for s in range(g * group, (g + 1) * group)], axis=0)
        if (g + 1) * group == sources:
            counts = jnp.where(counts > 0.0, counts, 1.0)
            averages = [part / counts for part in sums]
            norms = jnp.sum(averages[0] * averages[0] + averages[1] * averages[1], axis=1, keepdims=True)
            lengths = jnp.sqrt(norms + epsilon)
            centres = [part / lengths for part in averages]
            for f in range(2):
                for j in range(4):
                    for h in range(4):
                        row = 4 * (j % 2) + h
                        centre_ref[2 * (j // 2) + f, row : row + 1, :] = centres[f][j : j + 1, h * lanes : (h + 1) * lanes]
            centres = [part.astype(bf16) for part in centres]

            for s in range(sources):
                product = sum(
                    lax.dot_general(centres[f], block(s, f)[:reach], last_last, preferred_element_type=f32)
                    for f in range(2)
                )
                chosen = iota((8, reach), 0).astype(f32) == turn_ref[s : s + 1, :reach] - 1.0
                cosines.append(jnp.sum(jnp.where(chosen, product, 0.0), axis=0, keepdims=True))
        units = unit_ref[mine, :]
        near = pl.ds(0, (g + 1) * span)
        similar = lax.dot_general(units, unit_ref[near, :], last_last, preferred_element_type=f32)
        similar = jnp.where(turn_col == row_turn_ref[0:1, near], similar, -1.0)
        earlier = row_order_ref[0:1, near] < order_col
        best = jnp.max(jnp.where(earlier, similar, -1.0), axis=1, keepdims=True)
        if g:
            before = pl.ds(0, g * span)
            later = jnp.where(earlier[:, : g * span], -1.0, similar[:, : g * span])
            row_best_ref[0:1, before] = jnp.maximum(
                row_best_ref[0:1, before], jnp.max(later, axis=0, keepdims=True)
            )
        bests.append(best)

    table = jnp.zeros((reach, lanes), f32)
    lane_wide = iota((reach, lanes), 1)
    for s in range(sources):
        inverse = inverse_ref[s * slots : s * slots + reach, :]
        best = bests[s // group][(s % group) * slots : (s % group) * slots + reach]
        table = jnp.where(lane_wide == s, inverse, table)
        table = jnp.where(lane_wide == sources + s, best, table)
    if reach < lanes:
        table = jnp.concatenate([table, jnp.zeros((lanes - reach, lanes), f32)], axis=0)
        cosines = [jnp.concatenate([part, jnp.zeros((1, lanes - reach), f32)], axis=1) for part in cosines]
    across = table.T
    row_bests = [row_best_ref[0:1, s * slots : s * slots + reach] for s in range(sources)]
    if reach < lanes:
        filler = jnp.full((1, lanes - reach), -1.0, f32)
        row_bests = [jnp.concatenate([part, filler], axis=1) for part in row_bests]
    cosine = jnp.concatenate(cosines, axis=0) * across[:sources]
    best = jnp.maximum(across[sources : 2 * sources], jnp.concatenate(row_bests, axis=0))
    if spare:
        cosine = jnp.where(lane < cap, cosine, pltpu.roll(cosine, lanes - shift, 1))
        best = jnp.where(lane < cap, best, pltpu.roll(best, lanes - shift, 1))
    cosine_parts = split3(cosine)
    best_parts = split3(best)
    row = iota((8, lanes), 0)
    for s in range(sources):
        answer = jnp.zeros((8, lanes), f32)
        for t, part in enumerate(cosine_parts + best_parts):
            answer = jnp.where(row == t, part[s : s + 1], answer)
        for f in range(2):
            back_ref[2 * s + f] = jnp.concatenate([centre_ref[2 * (2 * s // sources) + f], answer], axis=1).astype(bf16)


def return_kernel(share, mine_ref, back_ref, info_ref, table_ref, centre_ref, cosine_ref, best_ref):
    dests = back_ref.shape[0]
    rows = info_ref.shape[1]
    step = 4 * lanes
    answers = back_ref[:, :, lanes:].reshape(dests * 8, lanes)
    for b in range(rows // step):
        at = pl.ds(b * step, step)
        dest = info_ref[0:1, at]
        position = info_ref[1:2, at]
        place = jnp.where(iota((lanes, step), 0) == position, 1.0, 0.0).astype(bf16)
        picked = jnp.dot(answers, place, preferred_element_type=f32)
        picked = jnp.where(iota((dests * 8, step), 0) // 8 == dest, picked, 0.0)
        picked = jnp.sum(picked.reshape(dests, 8, step), axis=0)
        cosine = picked[0:1] + picked[1:2] + picked[2:3]
        best = picked[3:4] + picked[4:5] + picked[5:6]
        for c in range(step // lanes):
            row = b * (step // lanes) + c
            cosine_ref[row : row + 1, :] = cosine[:, c * lanes : (c + 1) * lanes]
            best_ref[row : row + 1, :] = best[:, c * lanes : (c + 1) * lanes]
    owned = centre_ref.shape[0]
    code = table_ref[pl.ds(pl.multiple_of(mine_ref[0] * owned, 8), owned), :][:, :1]
    dest = code // share
    turn = code - dest * share
    stored = back_ref[:, :, :lanes].reshape(dests * 8, lanes)
    for h in range(4):
        want = dest * 8 + 4 * (turn % 2) + h
        hits = jnp.where(iota((owned, dests * 8), 1) == want, 1.0, 0.0).astype(bf16)
        centre_ref[:, h * lanes : (h + 1) * lanes] = jnp.dot(
            hits, stored, preferred_element_type=f32
        ).astype(bf16)


def vmem(count):
    return [pl.BlockSpec(memory_space=pltpu.VMEM)] * count


params = pltpu.CompilerParams(vmem_limit_bytes=50 * 1024 * 1024)


def exchange(x):
    return lax.all_to_all(x, AXES, split_axis=0, concat_axis=0, tiled=True)


def send(slots, spare, embeddings, assignments, order_index, cluster_blocks):
    dests = lax.axis_size("dp") * lax.axis_size("feat")
    rows, width = embeddings.shape
    clusters = cluster_blocks.shape[0]
    sent, info, table = pl.pallas_call(
        partial(pack_kernel, dests, slots, spare),
        out_shape=(
            jax.ShapeDtypeStruct((dests, slots, width), bf16),
            jax.ShapeDtypeStruct((8, rows), jnp.int32),
            jax.ShapeDtypeStruct((clusters, lanes), jnp.int32),
        ),
        in_specs=vmem(3) + [pl.BlockSpec(memory_space=pl.ANY)],
        out_specs=tuple(vmem(3)),
        scratch_shapes=[
            pltpu.VMEM((rows, width), bf16),
            pltpu.VMEM((4 * dests, rows), bf16),
            pltpu.VMEM((lanes, rows), bf16),
            pltpu.VMEM((-(-slots // 16) * 16, rows), bf16),
            pltpu.VMEM((dests, rows), f32),
            pltpu.SemaphoreType.DMA,
        ],
        compiler_params=params,
        name="pack",
    )(
        assignments.reshape(rows // lanes, lanes),
        order_index.reshape(rows // lanes, lanes),
        cluster_blocks.reshape(1, clusters),
        embeddings,
    )
    return exchange(sent), info, table


def answer(spare, got, info, table):
    n_dp = lax.axis_size("dp")
    dests, slots, width = got[0].shape
    total = n_dp * sum(part.shape[1] for part in got)
    rows = info.shape[1]
    back, level = pl.pallas_call(
        partial(owner_kernel, spare),
        out_shape=(
            jax.ShapeDtypeStruct((dests, 8, 2 * lanes), bf16),
            jax.ShapeDtypeStruct((8, lanes), jnp.int32),
        ),
        in_specs=vmem(len(got)),
        out_specs=tuple(vmem(2)),
        scratch_shapes=[
            pltpu.VMEM((total, 2 * width), bf16),
            pltpu.VMEM((total, 1), f32),
            pltpu.VMEM((lanes, lanes), f32),
            pltpu.VMEM((lanes, lanes), f32),
            pltpu.VMEM((1, total), f32),
            pltpu.VMEM((1, total), f32),
            pltpu.VMEM((1, total), f32),
            pltpu.VMEM((4, 8, lanes), f32),
        ],
        compiler_params=params,
        name="owner",
    )(*got)
    returned = exchange(back)
    mine = lax.axis_index("dp").reshape(1).astype(jnp.int32)
    centres, cosine, best = pl.pallas_call(
        partial(return_kernel, 4),
        out_shape=(
            jax.ShapeDtypeStruct((table.shape[0] // n_dp, width), bf16),
            jax.ShapeDtypeStruct((rows // lanes, lanes), f32),
            jax.ShapeDtypeStruct((rows // lanes, lanes), f32),
        ),
        in_specs=[pl.BlockSpec(memory_space=pltpu.SMEM)] + vmem(3),
        out_specs=tuple(vmem(3)),
        compiler_params=params,
        name="answers",
    )(mine, returned, info, table)
    return (centres, cosine.reshape(rows), best.reshape(rows)), level[0, 0]


def body(embeddings, assignments, order_index, cluster_blocks):
    n_dp = lax.axis_size("dp")
    dests = n_dp * lax.axis_size("feat")
    rows = assignments.shape[0]
    clusters = cluster_blocks.shape[0]
    most = (clusters // dests) * (2 * rows // clusters)
    args = (embeddings, assignments, order_index, cluster_blocks)
    few = -(-11 * most // 128) * 8
    got, info, table = send(few, 8, *args)
    outputs, level = answer(0, (got,), info, table)

    def with_sibling():
        more = lax.ppermute(got[:, few - 16 :], "dp", [(i, i ^ 1) for i in range(n_dp)])
        return answer(8, (got, more), info, table)[0]

    def with_all():
        got, info, table = send(most + 32, 0, *args)
        return answer(0, (got,), info, table)[0]

    return lax.switch(level, [lambda: outputs, with_sibling, with_all])


def solution(mesh):
    return jax.shard_map(
        body,
        mesh=mesh,
        in_specs=(P("dp", "feat"), P("dp"), P("dp"), P()),
        out_specs=(P("dp", "feat"), P("dp"), P("dp")),
        check_vma=False,
    )
```
